128 devices in a mesh: tile: 16 (over y, x), visit: 8 (over z, core).
Axes of the slice: x: 4, y: 4, z: 4, core: 2. Of those that a mesh axis runs over, the one named last changes fastest.
Arguments:
- pixels: bfloat16 [8, 224, 256, 128], P('visit', 'tile'), may hold values from -6 to 6
- dest_block: int32 [8, 224], P('visit', 'tile'), may hold values from 0 to 255, as said below
- phase_index: int32 [8, 224, 2], P('visit', 'tile'), may hold values from 0 to 15
- basis_row: bfloat16 [9, 31], replicated, may hold values from -1 to 1
- basis_col: bfloat16 [9, 31], replicated, may hold values from -1 to 1
- coefficients: float32 [8, 9], P('visit'), may hold values from -2 to 2
- visit_weight: float32 [8], replicated, may hold values from 0.25 to 4
Outputs:
- coadd: float32 [256, 32768], P('visit', 'tile')
The draws below stay inside these ranges and needn't reach their ends.
Inputs may be any that keep to these rules, and one draw needn't show every extreme that they name: `dest_block`: within one visit the pieces lie on distinct sky blocks. Of the 14 pieces of one visit in rows s * 14 to (s + 1) * 14 - 1, at most 2 lie on the blocks of one tile, and exactly 2 do for some tile.
All inputs are finite; a program needn't handle non-finite values.
Results may differ from the reference program's by a relative error of at most 0.017.
Values may be sent and summed in bfloat16 or wider, within the bound.
No kernel may reach another device: no remote copies, remote signals or barrier semaphores. Data moves between devices by JAX's collectives and lax.ppermute only.
A program may use at most 128 MiB of HBM per device.

```python
import math
import jax
import jax.numpy as jnp
from jax import lax

BLOCK = 128
TAPS = 31
NBASIS = 9
PHASES = 16
CAP = 2
H = 256
BPT = 16
PIECES = 14
VISITS = 8
SOURCES = 224
SKY = 256


def draw_dest_block(key, part):
    tile_count = SOURCES // PIECES

    def one_visit(visit_key):
        order_key, spot_key = jax.random.split(visit_key)
        tile_order = jax.random.permutation(order_key, tile_count)
        spots = jax.vmap(lambda sub_key: jax.random.permutation(sub_key, BPT))(jax.random.split(spot_key, tile_count))
        source = jnp.arange(SOURCES) // PIECES
        within = jnp.arange(SOURCES) % PIECES
        target_tile = tile_order[(source + within // CAP) % tile_count]
        return target_tile * BPT + spots[target_tile, within]
    return jax.vmap(one_visit)(jax.random.split(key, VISITS)).astype(jnp.int32)


def place_ends(values, key, least, top_value):
    spot = [jax.random.randint(jax.random.fold_in(key, axis), (), 0, length) for axis, length in enumerate(values.shape)]
    main_axis = values.shape.index(max(values.shape))
    neighbour = spot[:main_axis] + [(spot[main_axis] + 1) % values.shape[main_axis]] + spot[main_axis + 1:]
    return values.at[tuple(spot)].set(least).at[tuple(neighbour)].set(top_value)


def levels(own_key, extent, shards, smallest, top_value):
    factor_of = 1.0
    for dim, blocks in shards:
        steps = jax.random.uniform(jax.random.fold_in(jax.random.fold_in(own_key, 6), dim), (blocks,), jnp.float32, smallest / len(shards), top_value / len(shards))
        factor_of = factor_of * jnp.repeat(jnp.exp(steps), extent[dim] // blocks).reshape((-1,) + (1,) * (len(extent) - 1 - dim))
    return factor_of


def noise(key, shape, scale, bound, shards=(), kind=jnp.bfloat16):
    entries = scale * jax.random.normal(key, shape, jnp.float32)
    if shards:
        entries = entries * levels(key, shape, shards, -0.22, 0.18)
    return jnp.clip(entries, -bound, bound).astype(kind)


def setup_inputs(seed: int = 0) -> dict:
    splits = jax.random.split(jax.random.key(seed), 8)
    return {
        "pixels": noise(splits[0], (VISITS, SOURCES, H, BLOCK), 1.0, 6.0, ((0, 8), (1, 16))),
        "dest_block": draw_dest_block(jax.random.fold_in(splits[7], 71), 0),
        "phase_index": place_ends(jax.random.randint(splits[2], (VISITS, SOURCES, 2), 0, PHASES), jax.random.fold_in(splits[2], 1), 0, PHASES - 1).astype(jnp.int32),
        "basis_row": noise(splits[3], (NBASIS, TAPS), TAPS ** -0.5, 1.0),
        "basis_col": noise(splits[4], (NBASIS, TAPS), TAPS ** -0.5, 1.0),
        "coefficients": noise(splits[5], (VISITS, NBASIS), 0.35, 2.0, ((0, 8),), jnp.float32),
        "visit_weight": jnp.clip(jnp.exp(jax.random.uniform(splits[6], (VISITS,), jnp.float32, math.log(0.25), math.log(4.0))), 0.25, 4.0),
    }


def lanczos(phase_value):
    fraction = phase_value.astype(jnp.float32) / PHASES
    distance = jnp.arange(-3, 4).astype(jnp.float32) - fraction
    weights_raw = jnp.sinc(distance) * jnp.sinc(distance / 4.0)
    return weights_raw / jnp.sum(weights_raw)


def warp_piece(single_piece, row_phase, col_phase):
    height = single_piece.shape[0]
    row_taps = lanczos(row_phase)
    col_taps = lanczos(col_phase)
    padded = jnp.pad(single_piece.astype(jnp.float32), ((3, 3), (BLOCK + 3, BLOCK + 3)))
    across = col_taps[0] * padded[:, 0:3 * BLOCK]
    for tap_id in range(1, 7):
        across = across + col_taps[tap_id] * padded[:, tap_id:tap_id + 3 * BLOCK]
    vertical = row_taps[0] * across[0:height]
    for tap_id in range(1, 7):
        vertical = vertical + row_taps[tap_id] * across[tap_id:tap_id + height]
    return vertical.astype(jnp.bfloat16)


def psf_match(canvas_low, basis_row, basis_col, visit_coeffs):
    half_taps = TAPS // 2
    image = canvas_low.astype(jnp.float32)[None, None]
    row_kernel = basis_row.astype(jnp.float32)[:, None, :, None]
    rowconv = lax.conv_general_dilated(image, row_kernel, (1, 1), ((half_taps, half_taps), (0, 0)), precision=lax.Precision.HIGHEST)
    rowconv = lax.optimization_barrier(rowconv.astype(jnp.bfloat16)).astype(jnp.float32)
    col_kernel = basis_col.astype(jnp.float32)[:, None, None, :]
    colconv = lax.conv_general_dilated(rowconv, col_kernel, (1, 1), ((0, 0), (half_taps, half_taps)), feature_group_count=NBASIS, precision=lax.Precision.HIGHEST)
    return jnp.einsum('k,khw->hw', visit_coeffs, colconv[0])


def reference(pixels, dest_block, phase_index, basis_row, basis_col, coefficients, visit_weight):
    weight_sum = jnp.sum(visit_weight)
    canvas_width = (SKY + 2) * BLOCK
    coadd = jnp.zeros((H, SKY * BLOCK), jnp.float32)
    for visit_id in range(VISITS):
        def place(which, canvas):
            window = warp_piece(pixels[visit_id, which], phase_index[visit_id, which, 0], phase_index[visit_id, which, 1])
            offset = (dest_block[visit_id, which] * BLOCK).astype(jnp.int32)
            current = lax.dynamic_slice(canvas, (jnp.int32(0), offset), (H, 3 * BLOCK))
            return lax.dynamic_update_slice(canvas, current + window.astype(jnp.float32), (jnp.int32(0), offset))
        canvas = lax.fori_loop(0, SOURCES, place, jnp.zeros((H, canvas_width), jnp.float32))
        matched = psf_match(canvas.astype(jnp.bfloat16), basis_row, basis_col, coefficients[visit_id])
        coadd = coadd + (visit_weight[visit_id] / weight_sum) * matched[:, BLOCK:BLOCK + SKY * BLOCK]
    return coadd
```

```python
import jax
import jax.numpy as jnp
import numpy as np
from jax import lax
from jax.experimental import pallas as pl
from jax.experimental.pallas import tpu as pltpu
from jax.sharding import PartitionSpec as P

BLOCK = 128
TAPS = 31
HALF = 15
NBASIS = 9
PHASES = 16
PIECES = 14
H = 256
TILES = 16
STRIP = 16
STRIDE = 164
REACH = 18
COLS = 18 * BLOCK
META = PIECES * STRIDE
SKY = 256
F32 = jnp.float32
BF16 = jnp.bfloat16


def tap_table():
    fraction = np.arange(PHASES)[:, None] / PHASES
    distance = np.arange(-3, 4)[None, :] - fraction
    raw = np.sinc(distance) * np.sinc(distance / 4.0)
    return raw / raw.sum(1, keepdims=True)


def row_bases():
    table = np.zeros((PHASES, H), np.float32)
    taps = tap_table()
    for tap in range(7):
        table[:, (tap - 3) % H] = taps[:, tap]
    return table


def col_bases():
    table = np.zeros((PHASES, 3 * BLOCK), np.float32)
    table[:, :7] = tap_table()[:, ::-1]
    return table


def spread(basis, base, width, step):
    lanes = [(base + step * tap) % width for tap in range(TAPS)]
    placing = np.zeros((TAPS, width), np.float32)
    placing[np.arange(TAPS), lanes] = 1.0
    return jnp.dot(basis.astype(F32), placing, precision=lax.Precision.HIGHEST)


def contribute(phase, dest, coef, vw, row_tab, col_tab, rowb, colb, pix, out, call, rall, xbuf, zbuf):
    visit = lax.axis_index("visit")
    total = vw[0]
    for other in range(1, 8):
        total = total + vw[other]
    share = jnp.full((1, BLOCK), vw[visit], F32) / jnp.full((1, BLOCK), total, F32)

    y_of = lax.broadcasted_iota(jnp.int32, (H, H), 0)
    x_of = lax.broadcasted_iota(jnp.int32, (H, H), 1)
    gap = x_of - y_of
    near = jnp.abs(gap) <= HALF
    lag = lax.broadcasted_iota(jnp.int32, (H, BLOCK), 0) - lax.broadcasted_iota(jnp.int32, (H, BLOCK), 1)
    inside = (lag >= 64 - HALF) & (lag <= 64 + HALF)
    for k in range(NBASIS):
        base = jnp.broadcast_to(rowb[k : k + 1, :], (H, H))
        band = pltpu.roll(base, 0, 1, stride=1, stride_axis=0)
        rall[:, k * H : (k + 1) * H] = jnp.where(near, band, 0.0).astype(BF16)
        line = colb[k : k + 1, :] * (share * coef[0, k])
        band = pltpu.roll(jnp.broadcast_to(line, (H, BLOCK)), 0, 1, stride=1, stride_axis=0)
        call[:, k * BLOCK : (k + 1) * BLOCK] = jnp.where(inside, band, 0.0).astype(BF16)

    close = jnp.abs(gap) <= 3
    xbuf[...] = jnp.zeros_like(xbuf)
    for i in range(PIECES):
        base = jnp.broadcast_to(row_tab[pl.ds(phase[i, 0], 1), :], (H, H))
        row_op = pltpu.roll(base, 0, 1, stride=1, stride_axis=0)
        row_op = jnp.where(close, row_op, 0.0).astype(BF16)
        tall = jnp.dot(row_op, pix[0, i], preferred_element_type=F32).astype(BF16)
        start = STRIDE * i + HALF + 64
        block, offset = divmod(start, BLOCK)
        count = -(-(offset + BLOCK + 6) // BLOCK)
        base = pltpu.roll(jnp.broadcast_to(col_tab[pl.ds(phase[i, 1], 1), :], (8, 3 * BLOCK)), offset, 1)
        base = jnp.broadcast_to(base[:1], (BLOCK, 3 * BLOCK))
        col_op = pltpu.roll(base, 0, 1, stride=1, stride_axis=0)[:, : count * BLOCK].astype(BF16)
        window = jnp.dot(tall, col_op, preferred_element_type=F32).astype(BF16)
        span = slice(block * BLOCK, (block + count) * BLOCK)
        xbuf[:, span] = xbuf[:, span] + window

    rows = lax.broadcasted_iota(jnp.int32, (H, BLOCK), 0) % STRIP
    lanes = lax.broadcasted_iota(jnp.int32, (H, BLOCK), 1)
    mark = jnp.zeros((H, BLOCK), F32)
    for i in range(PIECES):
        mark = jnp.where(rows == i, dest[0, i].astype(F32), mark)
    mark = jnp.where(lanes >= META % BLOCK, mark, 0.0)

    def pair(p, carry):
        for side in range(2):
            at = pl.multiple_of(p * 2 * BLOCK + side * BLOCK, BLOCK)
            part = xbuf[:, pl.ds(at, 2 * BLOCK)]
            z = jnp.dot(part, call[...], preferred_element_type=F32).astype(BF16)
            for k in range(NBASIS):
                zbuf[k * H : (k + 1) * H, side * BLOCK : (side + 1) * BLOCK] = z[:, k * BLOCK : (k + 1) * BLOCK]
        got = jnp.dot(rall[...], zbuf[...], preferred_element_type=F32)
        at = pl.multiple_of(p * 2 * BLOCK, BLOCK)
        out[:, :, pl.ds(at, 2 * BLOCK)] = got.astype(BF16).reshape(TILES, STRIP, 2 * BLOCK)
        return carry

    lax.fori_loop(0, COLS // (2 * BLOCK), pair, 0)
    last = out[:, :, COLS - BLOCK :].astype(F32) + mark.reshape(TILES, STRIP, BLOCK)
    out[:, :, COLS - BLOCK :] = last.astype(BF16)


def place(dest, arr, send, keep, main, left, right):
    core = lax.rem(lax.axis_index("visit"), 2)
    for buf in (main, left, right):
        buf[...] = jnp.zeros_like(buf)
    lane = lax.broadcasted_iota(jnp.int32, (STRIP, BLOCK), 1)
    for i in range(PIECES):
        q, o = divmod(STRIDE * i + REACH, BLOCK)

        def one(s, carry, i=i, q=q, o=o):
            def turned(b):
                block = arr[s, :, b * BLOCK : (b + 1) * BLOCK].astype(F32)
                return pltpu.roll(block, (BLOCK - o) % BLOCK, 1)

            first, second = turned(q), turned(q + 1)
            body = jnp.where(lane < BLOCK - o, first, second)
            low = first
            if o < REACH:
                low = jnp.where(lane < BLOCK - o, turned(q - 1), first)
            low = jnp.where(lane >= BLOCK - REACH, low, 0.0)
            high = second
            if o + REACH > BLOCK:
                high = jnp.where(lane < BLOCK - o, second, turned(q + 2))
            high = jnp.where(lane < REACH, high, 0.0)
            d = dest[s, i]
            main[d + 1] = body.astype(BF16)
            left[d] = low.astype(BF16)
            right[d + 2] = high.astype(BF16)
            return carry

        lax.fori_loop(0, TILES, one, 0, unroll=4)

    step = 8

    def total(start):
        picked = [buf[pl.ds(start + 1, step)].astype(F32) for buf in (main, left, right)]
        return picked[0] + picked[1] + picked[2]

    def fill(j, carry):
        send[pl.ds(j * step, step)] = total((1 - core) * 128 + j * step).astype(BF16)
        keep[pl.ds(j * step, step)] = total(core * 128 + j * step)
        return carry

    lax.fori_loop(0, 128 // step, fill, 0, unroll=2)


def on_device(pixels, dest_block, phase_index, basis_row, basis_col, coefficients, visit_weight):
    smem = pl.BlockSpec(memory_space=pltpu.SMEM)
    vmem = pl.BlockSpec(memory_space=pltpu.VMEM)
    rowb = spread(basis_row, -HALF, H, 1)
    colb = spread(basis_col, -(64 - HALF), BLOCK, -1)
    sent = pl.pallas_call(
        contribute,
        out_shape=jax.ShapeDtypeStruct((TILES, STRIP, COLS), BF16),
        in_specs=[smem] * 4 + [vmem] * 5,
        out_specs=vmem,
        scratch_shapes=[
            pltpu.VMEM((H, NBASIS * BLOCK), BF16),
            pltpu.VMEM((H, NBASIS * H), BF16),
            pltpu.VMEM((H, COLS + BLOCK), BF16),
            pltpu.VMEM((NBASIS * H, 2 * BLOCK), BF16),
        ],
        compiler_params=pltpu.CompilerParams(vmem_limit_bytes=40 * 1024 * 1024),
    )(
        phase_index[0], dest_block, coefficients, visit_weight,
        jnp.asarray(row_bases()), jnp.asarray(col_bases()), rowb, colb, pixels,
    )
    arrived = lax.all_to_all(sent, "tile", split_axis=0, concat_axis=0, tiled=True)
    blocks = arrived[:, :PIECES, META].astype(jnp.int32)
    sends, keeps = pl.pallas_call(
        place,
        out_shape=(
            jax.ShapeDtypeStruct((128, STRIP, BLOCK), BF16),
            jax.ShapeDtypeStruct((128, STRIP, BLOCK), F32),
        ),
        in_specs=[smem, vmem],
        out_specs=(vmem, vmem),
        scratch_shapes=[pltpu.VMEM((SKY + 2, STRIP, BLOCK), BF16)] * 3,
        compiler_params=pltpu.CompilerParams(vmem_limit_bytes=40 * 1024 * 1024),
    )(blocks, arrived)
    other = lax.ppermute(sends, "visit", [(i, i ^ 1) for i in range(8)])
    both = (keeps + other.astype(F32)).astype(BF16).reshape(4, 32, STRIP, BLOCK)
    quarters = lax.all_to_all(
        both, "visit", split_axis=0, concat_axis=0, tiled=True,
        axis_index_groups=[[0, 2, 4, 6], [1, 3, 5, 7]],
    )
    summed = jnp.sum(quarters.astype(F32), 0).astype(BF16).reshape(2, 16, STRIP, BLOCK)
    odd = lax.axis_index("tile") % 2 == 1
    parts = [jnp.where(odd, summed[1 - h], summed[h]) for h in range(2)]

    def route(h):
        return [
            (r * 8 + z * 2 + c, (8 * c + 2 * z + (r + h) % 2) * 8 + r // 2)
            for r in range(16) for z in range(4) for c in range(2)
        ]

    got = [lax.ppermute(parts[h], ("tile", "visit"), route(h)) for h in range(2)]
    upper = jnp.where(odd, got[1], got[0])
    lower = jnp.where(odd, got[0], got[1])
    whole = jnp.concatenate([upper, lower], 1).astype(F32)
    return jnp.transpose(whole, (1, 0, 2)).reshape(32, 16 * BLOCK)


def solution(mesh):
    placed = (
        P("visit", "tile", None, None),
        P("visit", "tile"),
        P("visit", "tile", None),
        P(),
        P(),
        P("visit", None),
        P(),
    )
    return jax.shard_map(
        on_device, mesh=mesh, in_specs=placed, out_specs=P("visit", "tile"), check_vma=False
    )
```

```python
import jax
import jax.numpy as jnp
import numpy as np
from jax import lax
from jax.experimental import pallas as pl
from jax.experimental.pallas import tpu as pltpu
from jax.sharding import PartitionSpec as P

BLOCK = 128
TAPS = 31
HALF = 15
NBASIS = 9
PHASES = 16
PIECES = 14
H = 256
TILES = 16
STRIP = 16
STRIDE = 164
REACH = 18
COLS = 18 * BLOCK
META = PIECES * STRIDE
PAIRS = COLS // (2 * BLOCK)
SKY = 256
F32 = jnp.float32
BF16 = jnp.bfloat16


def tap_table():
    fraction = np.arange(PHASES)[:, None] / PHASES
    distance = np.arange(-3, 4)[None, :] - fraction
    raw = np.sinc(distance) * np.sinc(distance / 4.0)
    return raw / raw.sum(1, keepdims=True)


def bases():
    table = np.zeros((2 * PHASES, 3 * BLOCK), np.float32)
    taps = tap_table()
    for tap in range(7):
        table[:PHASES, (tap - 3) % H] = taps[:, tap]
        table[PHASES:, 6 - tap] = taps[:, tap]
    return table


def contribute(
    phase_in, dest_in, coef_in, vw_in, tab_in, brow_in, bcol_in, pix_in, out,
    phase, dest, coef, vw, tab, brow, bcol, pix, call, rall, xbuf, zbuf, sems, pix_sems,
):
    small = [
        pltpu.make_async_copy(source, target, sems.at[n])
        for n, (source, target) in enumerate(
            [
                (brow_in, brow), (bcol_in, bcol), (coef_in, coef), (vw_in, vw),
                (phase_in, phase), (tab_in, tab), (dest_in, dest),
            ]
        )
    ]
    for copy in small:
        copy.start()
    fetches = [
        pltpu.make_async_copy(pix_in.at[0, i], pix.at[i], pix_sems.at[i]) for i in range(PIECES)
    ]
    for copy in fetches:
        copy.start()

    y_of = lax.broadcasted_iota(jnp.int32, (H, H), 0)
    x_of = lax.broadcasted_iota(jnp.int32, (H, H), 1)
    gap = x_of - y_of
    near = jnp.abs(gap) <= HALF
    close = jnp.abs(gap) <= 3
    lag = lax.broadcasted_iota(jnp.int32, (H, BLOCK), 0) - lax.broadcasted_iota(jnp.int32, (H, BLOCK), 1)
    inside = (lag >= 64 - HALF) & (lag <= 64 + HALF)

    def placing(base, width, step):
        tap = lax.broadcasted_iota(jnp.int32, (TAPS, width), 0)
        lane = lax.broadcasted_iota(jnp.int32, (TAPS, width), 1)
        at = base + step * tap
        at = jnp.where(at < 0, at + width, at)
        return jnp.where(lane == at, 1.0, 0.0).astype(BF16)

    for copy in small:
        copy.wait()
    visit = lax.axis_index("visit")
    total = vw[0]
    for other in range(1, 8):
        total = total + vw[other]
    share = jnp.full((1, BLOCK), vw[visit], F32) / jnp.full((1, BLOCK), total, F32)
    rowb = jnp.dot(brow[...], placing(-HALF, H, 1), preferred_element_type=F32)
    colb = jnp.dot(bcol[...], placing(HALF - 64, BLOCK, -1), preferred_element_type=F32)
    for k in range(NBASIS):
        line = colb[k : k + 1, :] * (share * coef[0, k])
        band = pltpu.roll(jnp.broadcast_to(line, (H, BLOCK)), 0, 1, stride=1, stride_axis=0)
        call[:, k * BLOCK : (k + 1) * BLOCK] = jnp.where(inside, band, 0.0).astype(BF16)
    for k in range(NBASIS):
        base = jnp.broadcast_to(rowb[k : k + 1, :], (H, H))
        band = pltpu.roll(base, 0, 1, stride=1, stride_axis=0)
        rall[:, k * H : (k + 1) * H] = jnp.where(near, band, 0.0).astype(BF16)

    for copy in fetches:
        copy.wait()
    written = set()

    def warp(i):
        base = jnp.broadcast_to(tab[pl.ds(phase[0, i], 1), :H], (H, H))
        row_op = pltpu.roll(base, 0, 1, stride=1, stride_axis=0)
        row_op = jnp.where(close, row_op, 0.0).astype(BF16)
        tall = jnp.dot(row_op, pix[i], preferred_element_type=F32).astype(BF16)
        block, offset = divmod(STRIDE * i + HALF + 64, BLOCK)
        count = -(-(offset + BLOCK + 6) // BLOCK)
        base = jnp.broadcast_to(tab[pl.ds(PHASES + phase[1, i], 1), :], (8, 3 * BLOCK))
        base = jnp.broadcast_to(pltpu.roll(base, offset, 1)[:1], (BLOCK, 3 * BLOCK))
        col_op = pltpu.roll(base, 0, 1, stride=1, stride_axis=0)[:, : count * BLOCK].astype(BF16)
        window = jnp.dot(tall, col_op, preferred_element_type=F32).astype(BF16)
        for n in range(count):
            span = slice((block + n) * BLOCK, (block + n + 1) * BLOCK)
            part = window[:, n * BLOCK : (n + 1) * BLOCK]
            xbuf[:, span] = xbuf[:, span] + part if block + n in written else part
            written.add(block + n)

    def columns(p):
        for side in range(2):
            at = (2 * p + side) * BLOCK
            z = jnp.dot(xbuf[:, at : at + 2 * BLOCK], call[...], preferred_element_type=F32).astype(BF16)
            for k in range(NBASIS):
                zbuf[p % 2, k * H : (k + 1) * H, side * BLOCK : (side + 1) * BLOCK] = z[:, k * BLOCK : (k + 1) * BLOCK]

    def rows(p):
        got = jnp.dot(rall[...], zbuf[p % 2], preferred_element_type=F32)
        if p == PAIRS - 1:
            row = lax.broadcasted_iota(jnp.int32, (H, 2 * BLOCK), 0) % STRIP
            lane = lax.broadcasted_iota(jnp.int32, (H, 2 * BLOCK), 1)
            for i in range(PIECES):
                here = (row == i) & (lane >= META % (2 * BLOCK))
                got = jnp.where(here, dest[0, i].astype(F32), got)
        out[:, :, 2 * p * BLOCK : 2 * (p + 1) * BLOCK] = got.astype(BF16).reshape(TILES, STRIP, 2 * BLOCK)

    done = 0
    for p in range(PAIRS + 1):
        while done < PIECES and STRIDE * done + HALF + 64 < (2 * p + 3) * BLOCK:
            warp(done)
            done += 1
        if p < PAIRS:
            columns(p)
        if p > 0:
            rows(p - 1)


def place(dest, arr, send, keep, main, left, right):
    core = lax.rem(lax.axis_index("visit"), 2)
    for buf in (main, left, right):
        buf[...] = jnp.zeros_like(buf)
    lane = lax.broadcasted_iota(jnp.int32, (STRIP, BLOCK), 1)
    for i in range(PIECES):
        q, o = divmod(STRIDE * i + REACH, BLOCK)

        def one(s, carry, i=i, q=q, o=o):
            def turned(b):
                block = arr[s, :, b * BLOCK : (b + 1) * BLOCK].astype(F32)
                return pltpu.roll(block, (BLOCK - o) % BLOCK, 1)

            first, second = turned(q), turned(q + 1)
            body = jnp.where(lane < BLOCK - o, first, second)
            low = first
            if o < REACH:
                low = jnp.where(lane < BLOCK - o, turned(q - 1), first)
            low = jnp.where(lane >= BLOCK - REACH, low, 0.0)
            high = second
            if o + REACH > BLOCK:
                high = jnp.where(lane < BLOCK - o, second, turned(q + 2))
            high = jnp.where(lane < REACH, high, 0.0)
            d = dest[s, i]
            main[d + 1] = body.astype(BF16)
            left[d] = low.astype(BF16)
            right[d + 2] = high.astype(BF16)
            return carry

        lax.fori_loop(0, TILES, one, 0, unroll=TILES)

    step = 8

    def total(start):
        picked = [buf[pl.ds(start + 1, step)].astype(F32) for buf in (main, left, right)]
        return picked[0] + picked[1] + picked[2]

    def fill(j, carry):
        send[pl.ds(j * step, step)] = total((1 - core) * 128 + j * step).astype(BF16)
        keep[pl.ds(j * step, step)] = total(core * 128 + j * step)
        return carry

    lax.fori_loop(0, 128 // step, fill, 0, unroll=2)


def on_device(pixels, dest_block, phase_index, basis_row, basis_col, coefficients, visit_weight):
    smem = pl.BlockSpec(memory_space=pltpu.SMEM)
    vmem = pl.BlockSpec(memory_space=pltpu.VMEM)
    sent = pl.pallas_call(
        contribute,
        out_shape=jax.ShapeDtypeStruct((TILES, STRIP, COLS), BF16),
        in_specs=[pl.BlockSpec(memory_space=pltpu.HBM)] * 8,
        out_specs=vmem,
        scratch_shapes=[
            pltpu.SMEM((2, PIECES), jnp.int32),
            pltpu.SMEM((1, PIECES), jnp.int32),
            pltpu.SMEM((1, NBASIS), F32),
            pltpu.SMEM((8,), F32),
            pltpu.VMEM((2 * PHASES, 3 * BLOCK), F32),
            pltpu.VMEM((NBASIS, TAPS), BF16),
            pltpu.VMEM((NBASIS, TAPS), BF16),
            pltpu.VMEM((PIECES, H, BLOCK), BF16),
            pltpu.VMEM((H, NBASIS * BLOCK), BF16),
            pltpu.VMEM((H, NBASIS * H), BF16),
            pltpu.VMEM((H, COLS + BLOCK), BF16),
            pltpu.VMEM((2, NBASIS * H, 2 * BLOCK), BF16),
            pltpu.SemaphoreType.DMA((7,)),
            pltpu.SemaphoreType.DMA((PIECES,)),
        ],
        compiler_params=pltpu.CompilerParams(vmem_limit_bytes=60 * 1024 * 1024),
    )(
        phase_index[0].T, dest_block, coefficients, visit_weight,
        jnp.asarray(bases()), basis_row, basis_col, pixels,
    )
    arrived = lax.all_to_all(sent, "tile", split_axis=0, concat_axis=0, tiled=True)
    blocks = arrived[:, :PIECES, META].astype(jnp.int32)
    sends, keeps = pl.pallas_call(
        place,
        out_shape=(
            jax.ShapeDtypeStruct((128, STRIP, BLOCK), BF16),
            jax.ShapeDtypeStruct((128, STRIP, BLOCK), F32),
        ),
        in_specs=[smem, vmem],
        out_specs=(vmem, vmem),
        scratch_shapes=[pltpu.VMEM((SKY + 2, STRIP, BLOCK), BF16)] * 3,
        compiler_params=pltpu.CompilerParams(vmem_limit_bytes=40 * 1024 * 1024),
    )(blocks, arrived)
    other = lax.ppermute(sends, "visit", [(i, i ^ 1) for i in range(8)])
    both = (keeps + other.astype(F32)).astype(BF16).reshape(4, 32, STRIP, BLOCK)
    quarters = lax.all_to_all(
        both, "visit", split_axis=0, concat_axis=0, tiled=True,
        axis_index_groups=[[0, 2, 4, 6], [1, 3, 5, 7]],
    )
    summed = jnp.sum(quarters.astype(F32), 0).astype(BF16).reshape(2, 16, STRIP, BLOCK)
    odd = lax.axis_index("tile") % 2 == 1
    parts = [jnp.where(odd, summed[1 - h], summed[h]) for h in range(2)]

    def route(h):
        return [
            (r * 8 + z * 2 + c, (8 * c + 2 * z + (r + h) % 2) * 8 + r // 2)
            for r in range(16) for z in range(4) for c in range(2)
        ]

    got = [lax.ppermute(parts[h], ("tile", "visit"), route(h)) for h in range(2)]
    upper = jnp.where(odd, got[1], got[0])
    lower = jnp.where(odd, got[0], got[1])
    whole = jnp.concatenate([upper, lower], 1).astype(F32)
    return jnp.transpose(whole, (1, 0, 2)).reshape(32, 16 * BLOCK)


def solution(mesh):
    placed = (
        P("visit", "tile", None, None),
        P("visit", "tile"),
        P("visit", "tile", None),
        P(),
        P(),
        P("visit", None),
        P(),
    )
    return jax.shard_map(
        on_device, mesh=mesh, in_specs=placed, out_specs=P("visit", "tile"), check_vma=False
    )
```

```python
import jax
import jax.numpy as jnp
import numpy as np
from jax import lax
from jax.experimental import pallas as pl
from jax.experimental.pallas import tpu as pltpu
from jax.sharding import PartitionSpec as P

BLOCK = 128
TAPS = 31
HALF = 15
NBASIS = 9
PHASES = 16
PIECES = 14
H = 256
TILES = 16
STRIP = 16
STRIDE = 164
REACH = 18
COLS = 18 * BLOCK
META = PIECES * STRIDE
PAIRS = COLS // (2 * BLOCK)
FETCH = 7
SKY = 256
F32 = jnp.float32
BF16 = jnp.bfloat16


def tap_table():
    fraction = np.arange(PHASES)[:, None] / PHASES
    distance = np.arange(-3, 4)[None, :] - fraction
    raw = np.sinc(distance) * np.sinc(distance / 4.0)
    return raw / raw.sum(1, keepdims=True)


def bases():
    table = np.zeros((2 * PHASES, 3 * BLOCK), np.float32)
    taps = tap_table()
    for tap in range(7):
        table[:PHASES, (tap - 3) % H] = taps[:, tap]
        table[PHASES:, 6 - tap] = taps[:, tap]
    return table


def contribute(
    phase_in, dest_in, coef_in, vw_in, tab_in, brow_in, bcol_in, pix_in, out,
    phase, dest, coef, vw, tab, brow, bcol, pix, call, rall, xbuf, zbuf, sems, pix_sems,
):
    small = [
        pltpu.make_async_copy(source, target, sems.at[n])
        for n, (source, target) in enumerate(
            [
                (brow_in, brow), (bcol_in, bcol), (coef_in, coef), (vw_in, vw),
                (phase_in, phase), (tab_in, tab), (dest_in, dest),
            ]
        )
    ]
    for copy in small:
        copy.start()
    fetches = [
        pltpu.make_async_copy(pix_in.at[0, pl.ds(i, FETCH)], pix.at[pl.ds(i, FETCH)], pix_sems.at[i // FETCH])
        for i in range(0, PIECES, FETCH)
    ]
    for copy in fetches:
        copy.start()

    y_of = lax.broadcasted_iota(jnp.int32, (H, H), 0)
    x_of = lax.broadcasted_iota(jnp.int32, (H, H), 1)
    gap = x_of - y_of
    near = jnp.abs(gap) <= HALF
    close = jnp.abs(gap) <= 3
    lag = lax.broadcasted_iota(jnp.int32, (H, BLOCK), 0) - lax.broadcasted_iota(jnp.int32, (H, BLOCK), 1)
    inside = (lag >= 64 - HALF) & (lag <= 64 + HALF)

    def placing(base, width, step):
        tap = lax.broadcasted_iota(jnp.int32, (TAPS, width), 0)
        lane = lax.broadcasted_iota(jnp.int32, (TAPS, width), 1)
        at = base + step * tap
        at = jnp.where(at < 0, at + width, at)
        return jnp.where(lane == at, 1.0, 0.0).astype(BF16)

    for copy in small:
        copy.wait()
    visit = lax.axis_index("visit")
    total = vw[0]
    for other in range(1, 8):
        total = total + vw[other]
    share = jnp.full((1, BLOCK), vw[visit], F32) / jnp.full((1, BLOCK), total, F32)
    rowb = jnp.dot(brow[...], placing(-HALF, H, 1), preferred_element_type=F32)
    colb = jnp.dot(bcol[...], placing(HALF - 64, BLOCK, -1), preferred_element_type=F32)
    for k in range(NBASIS):
        line = colb[k : k + 1, :] * (share * coef[0, k])
        band = pltpu.roll(jnp.broadcast_to(line, (H, BLOCK)), 0, 1, stride=1, stride_axis=0)
        call[:, k * BLOCK : (k + 1) * BLOCK] = jnp.where(inside, band, 0.0).astype(BF16)
    for k in range(NBASIS):
        base = jnp.broadcast_to(rowb[k : k + 1, :], (H, H))
        band = pltpu.roll(base, 0, 1, stride=1, stride_axis=0)
        rall[:, k * H : (k + 1) * H] = jnp.where(near, band, 0.0).astype(BF16)

    for copy in fetches:
        copy.wait()
    written = set()

    def warp(i):
        base = jnp.broadcast_to(tab[pl.ds(phase[0, i], 1), :H], (H, H))
        row_op = pltpu.roll(base, 0, 1, stride=1, stride_axis=0)
        row_op = jnp.where(close, row_op, 0.0).astype(BF16)
        tall = jnp.dot(row_op, pix[i], preferred_element_type=F32).astype(BF16)
        block, offset = divmod(STRIDE * i + HALF + 64, BLOCK)
        count = -(-(offset + BLOCK + 6) // BLOCK)
        base = jnp.broadcast_to(tab[pl.ds(PHASES + phase[1, i], 1), :], (8, 3 * BLOCK))
        base = jnp.broadcast_to(pltpu.roll(base, offset, 1)[:1], (BLOCK, 3 * BLOCK))
        col_op = pltpu.roll(base, 0, 1, stride=1, stride_axis=0)[:, : count * BLOCK].astype(BF16)
        window = jnp.dot(tall, col_op, preferred_element_type=F32).astype(BF16)
        for n in range(count):
            span = slice((block + n) * BLOCK, (block + n + 1) * BLOCK)
            part = window[:, n * BLOCK : (n + 1) * BLOCK]
            xbuf[:, span] = xbuf[:, span] + part if block + n in written else part
            written.add(block + n)

    def columns(p):
        for side in range(2):
            at = (2 * p + side) * BLOCK
            z = jnp.dot(xbuf[:, at : at + 2 * BLOCK], call[...], preferred_element_type=F32).astype(BF16)
            for k in range(NBASIS):
                zbuf[p % 2, k * H : (k + 1) * H, side * BLOCK : (side + 1) * BLOCK] = z[:, k * BLOCK : (k + 1) * BLOCK]

    def rows(p):
        got = jnp.dot(rall[...], zbuf[p % 2], preferred_element_type=F32)
        for strip in range(TILES):
            z, x = divmod(strip, 4)
            halves = [got[64 * z + 32 * c + 8 * x : 64 * z + 32 * c + 8 * x + 8] for c in range(2)]
            both = jnp.concatenate(halves, 0)
            if p == PAIRS - 1:
                row = lax.broadcasted_iota(jnp.int32, (STRIP, 2 * BLOCK), 0)
                lane = lax.broadcasted_iota(jnp.int32, (STRIP, 2 * BLOCK), 1)
                mark = jnp.zeros((STRIP, 2 * BLOCK), F32)
                for i in range(PIECES):
                    mark = jnp.where(row == i, dest[0, i].astype(F32), mark)
                both = jnp.where(lane >= META % (2 * BLOCK), mark, both)
            out[strip, :, 2 * p * BLOCK : 2 * (p + 1) * BLOCK] = both.astype(BF16)

    done = 0
    for p in range(PAIRS + 1):
        while done < PIECES and STRIDE * done + HALF + 64 < (2 * p + 3) * BLOCK:
            warp(done)
            done += 1
        if p < PAIRS:
            columns(p)
        if p > 0:
            rows(p - 1)


def place(dest, arr, send, keep, *bufs):
    main, left, right = bufs[:4], bufs[4:8], bufs[8:]
    for buf in bufs:
        buf[...] = jnp.zeros_like(buf)
    lane = lax.broadcasted_iota(jnp.int32, (STRIP, BLOCK), 1)
    for i in range(PIECES):
        q, o = divmod(STRIDE * i + REACH, BLOCK)
        for s in range(TILES):
            z = s // 4

            def turned(b):
                block = arr[s, :, b * BLOCK : (b + 1) * BLOCK].astype(F32)
                return pltpu.roll(block, (BLOCK - o) % BLOCK, 1)

            first, second = turned(q), turned(q + 1)
            body = jnp.where(lane < BLOCK - o, first, second)
            low = first
            if o < REACH:
                low = jnp.where(lane < BLOCK - o, turned(q - 1), first)
            low = jnp.where(lane >= BLOCK - REACH, low, 0.0)
            high = second
            if o + REACH > BLOCK:
                high = jnp.where(lane < BLOCK - o, second, turned(q + 2))
            high = jnp.where(lane < REACH, high, 0.0)
            d = dest[s, i]
            main[z][d + 1] = body.astype(BF16)
            left[z][d] = low.astype(BF16)
            right[z][d + 2] = high.astype(BF16)

    upper = lax.rem(lax.axis_index("visit"), 2) == 1

    def fill(j, carry):
        for u in range(4):
            pair = j * 4 + u
            stays, goes = [], []
            for side in range(2):
                terms = [buf[2 * pair + side + 1].astype(F32) for buf in bufs]
                terms = [terms[n] + terms[n + 6] for n in range(6)]
                terms = [terms[n] + terms[n + 3] for n in range(3)]
                terms = [terms[0] + terms[1] + terms[2]]
                stays.append(jnp.where(upper, terms[0][8:], terms[0][:8]))
                goes.append(jnp.where(upper, terms[0][:8], terms[0][8:]))
            send[pair] = jnp.concatenate(goes, 0).astype(BF16)
            keep[pair] = jnp.concatenate(stays, 0)
        return carry

    lax.fori_loop(0, SKY // 8, fill, 0)


def gather(arr, out):
    for x in range(4):
        for u in range(8):
            terms = [arr[4 * y + x, u].astype(F32) for y in range(4)]
            total = (terms[0] + terms[1]) + (terms[2] + terms[3])
            for side in range(2):
                at = (2 * u + side) * BLOCK
                out[8 * x : 8 * x + 8, at : at + BLOCK] = total[8 * side : 8 * side + 8]


def on_device(pixels, dest_block, phase_index, basis_row, basis_col, coefficients, visit_weight):
    smem = pl.BlockSpec(memory_space=pltpu.SMEM)
    vmem = pl.BlockSpec(memory_space=pltpu.VMEM)
    sent = pl.pallas_call(
        contribute,
        out_shape=jax.ShapeDtypeStruct((TILES, STRIP, COLS), BF16),
        in_specs=[pl.BlockSpec(memory_space=pltpu.HBM)] * 8,
        out_specs=vmem,
        scratch_shapes=[
            pltpu.SMEM((2, PIECES), jnp.int32),
            pltpu.SMEM((1, PIECES), jnp.int32),
            pltpu.SMEM((1, NBASIS), F32),
            pltpu.SMEM((8,), F32),
            pltpu.VMEM((2 * PHASES, 3 * BLOCK), F32),
            pltpu.VMEM((NBASIS, TAPS), BF16),
            pltpu.VMEM((NBASIS, TAPS), BF16),
            pltpu.VMEM((PIECES, H, BLOCK), BF16),
            pltpu.VMEM((H, NBASIS * BLOCK), BF16),
            pltpu.VMEM((H, NBASIS * H), BF16),
            pltpu.VMEM((H, COLS + BLOCK), BF16),
            pltpu.VMEM((2, NBASIS * H, 2 * BLOCK), BF16),
            pltpu.SemaphoreType.DMA((7,)),
            pltpu.SemaphoreType.DMA((PIECES // FETCH,)),
        ],
        compiler_params=pltpu.CompilerParams(vmem_limit_bytes=60 * 1024 * 1024),
    )(
        phase_index[0].T, dest_block, coefficients, visit_weight,
        jnp.asarray(bases()), basis_row, basis_col, pixels,
    )
    groups = [
        [(4 * y + x) * 8 + 2 * z + c for z in range(4) for x in range(4)]
        for c in range(2) for y in range(4)
    ]
    arrived = lax.all_to_all(
        sent, ("tile", "visit"), split_axis=0, concat_axis=0, tiled=True, axis_index_groups=groups
    )
    blocks = arrived[:, :PIECES, META].astype(jnp.int32)
    sends, keeps = pl.pallas_call(
        place,
        out_shape=(
            jax.ShapeDtypeStruct((128, STRIP, BLOCK), BF16),
            jax.ShapeDtypeStruct((128, STRIP, BLOCK), F32),
        ),
        in_specs=[smem, vmem],
        out_specs=(vmem, vmem),
        scratch_shapes=[pltpu.VMEM((SKY + 2, STRIP, BLOCK), BF16)] * 12,
        compiler_params=pltpu.CompilerParams(vmem_limit_bytes=40 * 1024 * 1024),
    )(blocks, arrived)
    other = lax.ppermute(sends, "visit", [(i, i ^ 1) for i in range(8)])
    both = (keeps + other.astype(F32)).astype(BF16).reshape(TILES, 8, STRIP, BLOCK)
    parts = lax.all_to_all(both, "tile", split_axis=0, concat_axis=0, tiled=True)
    return pl.pallas_call(
        gather,
        out_shape=jax.ShapeDtypeStruct((32, 16 * BLOCK), F32),
        in_specs=[vmem],
        out_specs=vmem,
    )(parts)


def solution(mesh):
    placed = (
        P("visit", "tile", None, None),
        P("visit", "tile"),
        P("visit", "tile", None),
        P(),
        P(),
        P("visit", None),
        P(),
    )
    return jax.shard_map(
        on_device, mesh=mesh, in_specs=placed, out_specs=P("visit", "tile"), check_vma=False
    )
```

```python
import jax
import jax.numpy as jnp
import numpy as np
from jax import lax
from jax.experimental import pallas as pl
from jax.experimental.pallas import tpu as pltpu
from jax.sharding import PartitionSpec as P

BLOCK = 128
TAPS = 31
HALF = 15
NBASIS = 9
PHASES = 16
PIECES = 14
H = 256
TILES = 16
STRIP = 16
STRIDE = 164
REACH = 18
COLS = 18 * BLOCK
META = PIECES * STRIDE
PAIRS = COLS // (2 * BLOCK)
FETCH = 7
SKY = 256
F32 = jnp.float32
BF16 = jnp.bfloat16


def tap_table():
    fraction = np.arange(PHASES)[:, None] / PHASES
    distance = np.arange(-3, 4)[None, :] - fraction
    raw = np.sinc(distance) * np.sinc(distance / 4.0)
    return raw / raw.sum(1, keepdims=True)


def bases():
    table = np.zeros((2 * PHASES, 3 * BLOCK), np.float32)
    taps = tap_table()
    for tap in range(7):
        table[:PHASES, (tap - 3) % H] = taps[:, tap]
        table[PHASES:, 6 - tap] = taps[:, tap]
    return table


def contribute(
    phase_in, dest_in, coef_in, vw_in, tab_in, brow_in, bcol_in, pix_in, out,
    phase, dest, coef, vw, tab, brow, bcol, pix, call, rall, xbuf, zbuf, sems, pix_sems,
):
    small = [
        pltpu.make_async_copy(source, target, sems.at[n])
        for n, (source, target) in enumerate(
            [
                (brow_in, brow), (bcol_in, bcol), (coef_in, coef), (vw_in, vw),
                (phase_in, phase), (tab_in, tab), (dest_in, dest),
            ]
        )
    ]
    for copy in small:
        copy.start()
    fetches = [
        pltpu.make_async_copy(pix_in.at[0, pl.ds(i, FETCH)], pix.at[pl.ds(i, FETCH)], pix_sems.at[i // FETCH])
        for i in range(0, PIECES, FETCH)
    ]
    for copy in fetches:
        copy.start()

    y_of = lax.broadcasted_iota(jnp.int32, (H, H), 0)
    x_of = lax.broadcasted_iota(jnp.int32, (H, H), 1)
    gap = x_of - y_of
    near = jnp.abs(gap) <= HALF
    close = jnp.abs(gap) <= 3
    lag = lax.broadcasted_iota(jnp.int32, (H, BLOCK), 0) - lax.broadcasted_iota(jnp.int32, (H, BLOCK), 1)
    inside = (lag >= 64 - HALF) & (lag <= 64 + HALF)

    def placing(base, width, step):
        tap = lax.broadcasted_iota(jnp.int32, (TAPS, width), 0)
        lane = lax.broadcasted_iota(jnp.int32, (TAPS, width), 1)
        at = base + step * tap
        at = jnp.where(at < 0, at + width, at)
        return jnp.where(lane == at, 1.0, 0.0).astype(BF16)

    for copy in small:
        copy.wait()
    visit = lax.axis_index("visit")
    total = vw[0]
    for other in range(1, 8):
        total = total + vw[other]
    share = jnp.full((1, BLOCK), vw[visit], F32) / jnp.full((1, BLOCK), total, F32)
    rowb = jnp.dot(brow[...], placing(-HALF, H, 1), preferred_element_type=F32)
    colb = jnp.dot(bcol[...], placing(HALF - 64, BLOCK, -1), preferred_element_type=F32)
    for k in range(NBASIS):
        line = colb[k : k + 1, :] * (share * coef[0, k])
        band = pltpu.roll(jnp.broadcast_to(line, (H, BLOCK)), 0, 1, stride=1, stride_axis=0)
        call[:, k * BLOCK : (k + 1) * BLOCK] = jnp.where(inside, band, 0.0).astype(BF16)
    for k in range(NBASIS):
        base = jnp.broadcast_to(rowb[k : k + 1, :], (H, H))
        band = pltpu.roll(base, 0, 1, stride=1, stride_axis=0)
        rall[:, k * H : (k + 1) * H] = jnp.where(near, band, 0.0).astype(BF16)

    for copy in fetches:
        copy.wait()
    written = set()

    def warp(i):
        base = jnp.broadcast_to(tab[pl.ds(phase[0, i], 1), :H], (H, H))
        row_op = pltpu.roll(base, 0, 1, stride=1, stride_axis=0)
        row_op = jnp.where(close, row_op, 0.0).astype(BF16)
        tall = jnp.dot(row_op, pix[i], preferred_element_type=F32).astype(BF16)
        block, offset = divmod(STRIDE * i + HALF + 64, BLOCK)
        count = -(-(offset + BLOCK + 6) // BLOCK)
        base = jnp.broadcast_to(tab[pl.ds(PHASES + phase[1, i], 1), :], (8, 3 * BLOCK))
        base = jnp.broadcast_to(pltpu.roll(base, offset, 1)[:1], (BLOCK, 3 * BLOCK))
        col_op = pltpu.roll(base, 0, 1, stride=1, stride_axis=0)[:, : count * BLOCK].astype(BF16)
        window = jnp.dot(tall, col_op, preferred_element_type=F32).astype(BF16)
        for n in range(count):
            span = slice((block + n) * BLOCK, (block + n + 1) * BLOCK)
            part = window[:, n * BLOCK : (n + 1) * BLOCK]
            xbuf[:, span] = xbuf[:, span] + part if block + n in written else part
            written.add(block + n)

    def columns(p):
        for side in range(2):
            at = (2 * p + side) * BLOCK
            z = jnp.dot(xbuf[:, at : at + 2 * BLOCK], call[...], preferred_element_type=F32).astype(BF16)
            for k in range(NBASIS):
                zbuf[p % 2, k * H : (k + 1) * H, side * BLOCK : (side + 1) * BLOCK] = z[:, k * BLOCK : (k + 1) * BLOCK]

    def rows(p):
        got = jnp.dot(rall[...], zbuf[p % 2], preferred_element_type=F32)
        for strip in range(TILES):
            z, x = divmod(strip, 4)
            halves = [got[64 * z + 32 * c + 8 * x : 64 * z + 32 * c + 8 * x + 8] for c in range(2)]
            both = jnp.concatenate(halves, 0)
            if p == PAIRS - 1:
                row = lax.broadcasted_iota(jnp.int32, (STRIP, 2 * BLOCK), 0)
                lane = lax.broadcasted_iota(jnp.int32, (STRIP, 2 * BLOCK), 1)
                mark = jnp.zeros((STRIP, 2 * BLOCK), F32)
                for i in range(PIECES):
                    mark = jnp.where(row == i, dest[0, i].astype(F32), mark)
                both = jnp.where(lane >= META % (2 * BLOCK), mark, both)
            out[strip, :, 2 * p * BLOCK : 2 * (p + 1) * BLOCK] = both.astype(BF16)

    done = 0
    for p in range(PAIRS + 1):
        while done < PIECES and STRIDE * done + HALF + 64 < (2 * p + 3) * BLOCK:
            warp(done)
            done += 1
        if p < PAIRS:
            columns(p)
        if p > 0:
            rows(p - 1)


def place(dest, arr, send, keep, *bufs):
    main, left, right = bufs
    for buf in bufs:
        buf[...] = jnp.zeros_like(buf)
    lane = lax.broadcasted_iota(jnp.int32, (STRIP, BLOCK), 1)
    for s in range(TILES):
        z = s // 4
        for i in range(PIECES):
            q, o = divmod(STRIDE * i + REACH, BLOCK)

            def turned(b):
                block = arr[s, :, b * BLOCK : (b + 1) * BLOCK].astype(F32)
                return pltpu.roll(block, (BLOCK - o) % BLOCK, 1)

            first, second = turned(q), turned(q + 1)
            body = jnp.where(lane < BLOCK - o, first, second)
            low = first
            if o < REACH:
                low = jnp.where(lane < BLOCK - o, turned(q - 1), first)
            low = jnp.where(lane >= BLOCK - REACH, low, 0.0)
            high = second
            if o + REACH > BLOCK:
                high = jnp.where(lane < BLOCK - o, second, turned(q + 2))
            high = jnp.where(lane < REACH, high, 0.0)
            d = dest[s, i]
            for buf, at, part in ((main, d + 1, body), (left, d, low), (right, d + 2, high)):
                buf[at] = part if z == 0 else buf[at] + part

    upper = lax.rem(lax.axis_index("visit"), 2) == 1

    def fill(j, carry):
        for u in range(4):
            pair = j * 4 + u
            stays, goes = [], []
            for side in range(2):
                total = main[2 * pair + side + 1] + left[2 * pair + side + 1] + right[2 * pair + side + 1]
                stays.append(jnp.where(upper, total[8:], total[:8]))
                goes.append(jnp.where(upper, total[:8], total[8:]))
            send[pair] = jnp.concatenate(goes, 0).astype(BF16)
            keep[pair] = jnp.concatenate(stays, 0)
        return carry

    lax.fori_loop(0, SKY // 8, fill, 0, unroll=2)


def gather(arr, out):
    for x in range(4):
        for u in range(8):
            terms = [arr[4 * y + x, u].astype(F32) for y in range(4)]
            total = (terms[0] + terms[1]) + (terms[2] + terms[3])
            for side in range(2):
                at = (2 * u + side) * BLOCK
                out[8 * x : 8 * x + 8, at : at + BLOCK] = total[8 * side : 8 * side + 8]


def on_device(pixels, dest_block, phase_index, basis_row, basis_col, coefficients, visit_weight):
    smem = pl.BlockSpec(memory_space=pltpu.SMEM)
    vmem = pl.BlockSpec(memory_space=pltpu.VMEM)
    sent = pl.pallas_call(
        contribute,
        out_shape=jax.ShapeDtypeStruct((TILES, STRIP, COLS), BF16),
        in_specs=[pl.BlockSpec(memory_space=pltpu.HBM)] * 8,
        out_specs=vmem,
        scratch_shapes=[
            pltpu.SMEM((2, PIECES), jnp.int32),
            pltpu.SMEM((1, PIECES), jnp.int32),
            pltpu.SMEM((1, NBASIS), F32),
            pltpu.SMEM((8,), F32),
            pltpu.VMEM((2 * PHASES, 3 * BLOCK), F32),
            pltpu.VMEM((NBASIS, TAPS), BF16),
            pltpu.VMEM((NBASIS, TAPS), BF16),
            pltpu.VMEM((PIECES, H, BLOCK), BF16),
            pltpu.VMEM((H, NBASIS * BLOCK), BF16),
            pltpu.VMEM((H, NBASIS * H), BF16),
            pltpu.VMEM((H, COLS + BLOCK), BF16),
            pltpu.VMEM((2, NBASIS * H, 2 * BLOCK), BF16),
            pltpu.SemaphoreType.DMA((7,)),
            pltpu.SemaphoreType.DMA((PIECES // FETCH,)),
        ],
        compiler_params=pltpu.CompilerParams(vmem_limit_bytes=60 * 1024 * 1024),
    )(
        phase_index[0].T, dest_block, coefficients, visit_weight,
        jnp.asarray(bases()), basis_row, basis_col, pixels,
    )
    groups = [
        [(4 * y + x) * 8 + 2 * z + c for z in range(4) for x in range(4)]
        for c in range(2) for y in range(4)
    ]
    arrived = lax.all_to_all(
        sent, ("tile", "visit"), split_axis=0, concat_axis=0, tiled=True, axis_index_groups=groups
    )
    blocks = arrived[:, :PIECES, META].astype(jnp.int32)
    sends, keeps = pl.pallas_call(
        place,
        out_shape=(
            jax.ShapeDtypeStruct((128, STRIP, BLOCK), BF16),
            jax.ShapeDtypeStruct((128, STRIP, BLOCK), F32),
        ),
        in_specs=[smem, vmem],
        out_specs=(vmem, vmem),
        scratch_shapes=[pltpu.VMEM((SKY + 2, STRIP, BLOCK), F32)] * 3,
        compiler_params=pltpu.CompilerParams(vmem_limit_bytes=40 * 1024 * 1024),
    )(blocks, arrived)
    other = lax.ppermute(sends, "visit", [(i, i ^ 1) for i in range(8)])
    both = (keeps + other.astype(F32)).astype(BF16).reshape(TILES, 8, STRIP, BLOCK)
    parts = lax.all_to_all(both, "tile", split_axis=0, concat_axis=0, tiled=True)
    return pl.pallas_call(
        gather,
        out_shape=jax.ShapeDtypeStruct((32, 16 * BLOCK), F32),
        in_specs=[vmem],
        out_specs=vmem,
        compiler_params=pltpu.CompilerParams(vmem_limit_bytes=16 * 1024 * 1024),
    )(parts)


def solution(mesh):
    placed = (
        P("visit", "tile", None, None),
        P("visit", "tile"),
        P("visit", "tile", None),
        P(),
        P(),
        P("visit", None),
        P(),
    )
    return jax.shard_map(
        on_device, mesh=mesh, in_specs=placed, out_specs=P("visit", "tile"), check_vma=False
    )
```

```python
import jax
import jax.numpy as jnp
import numpy as np
from jax import lax
from jax.experimental import pallas as pl
from jax.experimental.pallas import tpu as pltpu
from jax.sharding import PartitionSpec as P

BLOCK = 128
TAPS = 31
HALF = 15
NBASIS = 9
PHASES = 16
PIECES = 14
H = 256
TILES = 16
STRIP = 16
STRIDE = 164
REACH = 18
COLS = 18 * BLOCK
META = PIECES * STRIDE
PAIRS = COLS // (2 * BLOCK)
FETCH = 7
AHEAD = 6
NEED = 144
DEPTH = NBASIS * NEED
SKY = 256
F32 = jnp.float32
BF16 = jnp.bfloat16


def tap_table():
    fraction = np.arange(PHASES)[:, None] / PHASES
    distance = np.arange(-3, 4)[None, :] - fraction
    raw = np.sinc(distance) * np.sinc(distance / 4.0)
    return raw / raw.sum(1, keepdims=True)


def bases():
    table = np.zeros((2 * PHASES, 3 * BLOCK), np.float32)
    taps = tap_table()
    for tap in range(7):
        table[:PHASES, (tap - 3) % BLOCK] = taps[:, tap]
        table[PHASES:, 6 - tap] = taps[:, tap]
    return table


def contribute(
    phase_in, dest_in, coef_in, vw_in, tab_in, brow_in, bcol_in, pix_in, out,
    phase, dest, coef, vw, tab, brow, bcol, pix, call, rall, xbuf, zbuf, sems, pix_sems,
):
    small = [
        pltpu.make_async_copy(source, target, sems.at[n])
        for n, (source, target) in enumerate(
            [
                (brow_in, brow), (bcol_in, bcol), (coef_in, coef), (vw_in, vw),
                (phase_in, phase), (tab_in, tab), (dest_in, dest),
            ]
        )
    ]
    for copy in small:
        copy.start()
    fetches = [
        pltpu.make_async_copy(pix_in.at[0, pl.ds(i, FETCH)], pix.at[pl.ds(i, FETCH)], pix_sems.at[i // FETCH])
        for i in range(0, PIECES, FETCH)
    ]
    for copy in fetches:
        copy.start()

    edge = lax.broadcasted_iota(jnp.int32, (8, BLOCK), 1)
    blank = jnp.zeros((BLOCK - 8, BLOCK), F32)
    lag = lax.broadcasted_iota(jnp.int32, (H, BLOCK), 0) - lax.broadcasted_iota(jnp.int32, (H, BLOCK), 1)
    inside = (lag >= 64 - HALF) & (lag <= 64 + HALF)

    def placing(base, width, step):
        tap = lax.broadcasted_iota(jnp.int32, (TAPS, width), 0)
        lane = lax.broadcasted_iota(jnp.int32, (TAPS, width), 1)
        at = base + step * tap
        at = jnp.where(at < 0, at + width, at)
        return jnp.where(lane == at, 1.0, 0.0).astype(BF16)

    for copy in small:
        copy.wait()
    visit = lax.axis_index("visit")
    total = vw[0]
    for other in range(1, 8):
        total = total + vw[other]
    share = jnp.full((1, BLOCK), vw[visit], F32) / jnp.full((1, BLOCK), total, F32)
    rowb = jnp.dot(brow[...], placing(-HALF, H, 1), preferred_element_type=F32)
    colb = jnp.dot(bcol[...], placing(HALF - 64, BLOCK, -1), preferred_element_type=F32)
    for k in range(NBASIS):
        line = colb[k : k + 1, :] * (share * coef[0, k])
        band = pltpu.roll(jnp.broadcast_to(line, (H, BLOCK)), 0, 1, stride=1, stride_axis=0)
        call[:, k * BLOCK : (k + 1) * BLOCK] = jnp.where(inside, band, 0.0).astype(BF16)
    for copy in fetches:
        copy.wait()
    written = set()
    talls = {}

    def lift(i):
        base = jnp.broadcast_to(tab[pl.ds(phase[0, i], 1), :][:, :BLOCK], (BLOCK, BLOCK))
        ring = pltpu.roll(base, 0, 1, stride=1, stride_axis=0)
        top, bottom = ring[:8], ring[120:]
        inner = jnp.concatenate(
            [jnp.where(edge >= 64, 0.0, top), ring[8:120], jnp.where(edge < 64, 0.0, bottom)], 0
        ).astype(BF16)
        beyond = jnp.concatenate([blank, jnp.where(edge < 64, bottom, 0.0)], 0).astype(BF16)
        before = jnp.concatenate([jnp.where(edge >= 64, top, 0.0), blank], 0).astype(BF16)
        row_op = jnp.concatenate(
            [jnp.concatenate([inner, beyond], 1), jnp.concatenate([before, inner], 1)], 0
        )
        talls[i] = jnp.dot(row_op, pix[i], preferred_element_type=F32).astype(BF16)

    def warp(i):
        if i + AHEAD < PIECES:
            lift(i + AHEAD)
        tall = talls.pop(i)
        block, offset = divmod(STRIDE * i + HALF + 64, BLOCK)
        count = -(-(offset + BLOCK + 6) // BLOCK)
        base = jnp.broadcast_to(tab[pl.ds(PHASES + phase[1, i], 1), :][:, : count * BLOCK], (8, count * BLOCK))
        base = jnp.broadcast_to(pltpu.roll(base, offset, 1)[:1], (BLOCK, count * BLOCK))
        col_op = pltpu.roll(base, 0, 1, stride=1, stride_axis=0).astype(BF16)
        window = jnp.dot(tall, col_op, preferred_element_type=F32).astype(BF16)
        for n in range(count):
            span = slice((block + n) * BLOCK, (block + n + 1) * BLOCK)
            part = window[:, n * BLOCK : (n + 1) * BLOCK]
            xbuf[:, span] = xbuf[:, span] + part if block + n in written else part
            written.add(block + n)

    def columns(p):
        for side in range(2):
            at = (2 * p + side) * BLOCK
            z = jnp.dot(xbuf[:, at : at + 2 * BLOCK], call[...], preferred_element_type=F32).astype(BF16)
            for k in range(NBASIS):
                zk = z[:, k * BLOCK : (k + 1) * BLOCK]
                for h in range(2):
                    at = DEPTH * h + NEED * k
                    zbuf[p % 2, at : at + NEED, side * BLOCK : (side + 1) * BLOCK] = zk[112 * h : 112 * h + NEED]

    def rows(p):
        got = [
            jnp.dot(
                rall[h, :, :DEPTH], zbuf[p % 2, DEPTH * h : DEPTH * (h + 1)], preferred_element_type=F32
            )
            for h in range(2)
        ]
        for strip in range(TILES):
            z, x = divmod(strip, 4)
            first = 64 * (z % 2) + 8 * x
            halves = [got[z // 2][first + 32 * c : first + 32 * c + 8] for c in range(2)]
            both = jnp.concatenate(halves, 0)
            if p == PAIRS - 1:
                row = lax.broadcasted_iota(jnp.int32, (STRIP, 2 * BLOCK), 0)
                lane = lax.broadcasted_iota(jnp.int32, (STRIP, 2 * BLOCK), 1)
                mark = jnp.zeros((STRIP, 2 * BLOCK), F32)
                for i in range(PIECES):
                    mark = jnp.where(row == i, dest[0, i].astype(F32), mark)
                both = jnp.where(lane >= META % (2 * BLOCK), mark, both)
            out[strip, :, 2 * p * BLOCK : 2 * (p + 1) * BLOCK] = both.astype(BF16)

    def rbuild():
        lane = lax.broadcasted_iota(jnp.int32, (BLOCK, H), 1)
        for h in range(2):
            for k in range(NBASIS):
                block, offset = divmod(NEED * k, BLOCK)
                base = jnp.broadcast_to(rowb[k : k + 1, :], (8, H))
                base = pltpu.roll(base, offset + STRIP * h, 1)
                band = pltpu.roll(jnp.broadcast_to(base[:1], (BLOCK, H)), 0, 1, stride=1, stride_axis=0)
                band = jnp.where((lane >= offset) & (lane < offset + NEED), band, 0.0).astype(BF16)
                for n in range(2):
                    span = slice((block + n) * BLOCK, (block + n + 1) * BLOCK)
                    part = band[:, n * BLOCK : (n + 1) * BLOCK]
                    rall[h, :, span] = rall[h, :, span] + part if n == 0 and offset else part

    def ready(p):
        while len(warped) < PIECES and STRIDE * len(warped) + HALF + 64 < (2 * p + 3) * BLOCK:
            warp(len(warped))
            warped.append(True)

    warped = []
    for i in range(AHEAD):
        lift(i)
    ready(0)
    for p in range(PAIRS + 1):
        if p < PAIRS:
            columns(p)
        if p == 0:
            rbuild()
        if p + 1 < PAIRS:
            ready(p + 1)
        if p > 0:
            rows(p - 1)


def place(dest, arr, send, keep, *bufs):
    main, left, right = bufs
    for buf in bufs:
        buf[...] = jnp.zeros_like(buf)
    lane = lax.broadcasted_iota(jnp.int32, (STRIP, BLOCK), 1)
    for s in range(TILES):
        z = s // 4
        for i in range(PIECES):
            q, o = divmod(STRIDE * i + REACH, BLOCK)

            def turned(b):
                block = arr[s, :, b * BLOCK : (b + 1) * BLOCK].astype(F32)
                return pltpu.roll(block, (BLOCK - o) % BLOCK, 1)

            first, second = turned(q), turned(q + 1)
            body = jnp.where(lane < BLOCK - o, first, second)
            low = first
            if o < REACH:
                low = jnp.where(lane < BLOCK - o, turned(q - 1), first)
            low = jnp.where(lane >= BLOCK - REACH, low, 0.0)
            high = second
            if o + REACH > BLOCK:
                high = jnp.where(lane < BLOCK - o, second, turned(q + 2))
            high = jnp.where(lane < REACH, high, 0.0)
            d = dest[s, i]
            for buf, at, part in ((main, d + 1, body), (left, d, low), (right, d + 2, high)):
                buf[at] = part if z == 0 else buf[at] + part

    upper = lax.rem(lax.axis_index("visit"), 2) == 1

    def fill(j, carry):
        for u in range(4):
            pair = j * 4 + u
            stays, goes = [], []
            for side in range(2):
                total = main[2 * pair + side + 1] + left[2 * pair + side + 1] + right[2 * pair + side + 1]
                stays.append(jnp.where(upper, total[8:], total[:8]))
                goes.append(jnp.where(upper, total[:8], total[8:]))
            send[pair] = jnp.concatenate(goes, 0).astype(BF16)
            keep[pair] = jnp.concatenate(stays, 0)
        return carry

    lax.fori_loop(0, SKY // 8, fill, 0, unroll=2)


def gather(arr, out):
    for x in range(4):
        for u in range(8):
            terms = [arr[4 * y + x, u].astype(F32) for y in range(4)]
            total = (terms[0] + terms[1]) + (terms[2] + terms[3])
            for side in range(2):
                at = (2 * u + side) * BLOCK
                out[8 * x : 8 * x + 8, at : at + BLOCK] = total[8 * side : 8 * side + 8]


def on_device(pixels, dest_block, phase_index, basis_row, basis_col, coefficients, visit_weight):
    smem = pl.BlockSpec(memory_space=pltpu.SMEM)
    vmem = pl.BlockSpec(memory_space=pltpu.VMEM)
    sent = pl.pallas_call(
        contribute,
        out_shape=jax.ShapeDtypeStruct((TILES, STRIP, COLS), BF16),
        in_specs=[pl.BlockSpec(memory_space=pltpu.HBM)] * 8,
        out_specs=vmem,
        scratch_shapes=[
            pltpu.SMEM((2, PIECES), jnp.int32),
            pltpu.SMEM((1, PIECES), jnp.int32),
            pltpu.SMEM((1, NBASIS), F32),
            pltpu.SMEM((8,), F32),
            pltpu.VMEM((2 * PHASES, 3 * BLOCK), F32),
            pltpu.VMEM((NBASIS, TAPS), BF16),
            pltpu.VMEM((NBASIS, TAPS), BF16),
            pltpu.VMEM((PIECES, H, BLOCK), BF16),
            pltpu.VMEM((H, NBASIS * BLOCK), BF16),
            pltpu.VMEM((2, BLOCK, 11 * BLOCK), BF16),
            pltpu.VMEM((H, COLS + BLOCK), BF16),
            pltpu.VMEM((2, 2 * DEPTH, 2 * BLOCK), BF16),
            pltpu.SemaphoreType.DMA((7,)),
            pltpu.SemaphoreType.DMA((PIECES // FETCH,)),
        ],
        compiler_params=pltpu.CompilerParams(vmem_limit_bytes=60 * 1024 * 1024),
    )(
        phase_index[0].T, dest_block, coefficients, visit_weight,
        jnp.asarray(bases()), basis_row, basis_col, pixels,
    )
    groups = [
        [(4 * y + x) * 8 + 2 * z + c for z in range(4) for x in range(4)]
        for c in range(2) for y in range(4)
    ]
    arrived = lax.all_to_all(
        sent, ("tile", "visit"), split_axis=0, concat_axis=0, tiled=True, axis_index_groups=groups
    )
    blocks = arrived[:, :PIECES, META].astype(jnp.int32)
    sends, keeps = pl.pallas_call(
        place,
        out_shape=(
            jax.ShapeDtypeStruct((128, STRIP, BLOCK), BF16),
            jax.ShapeDtypeStruct((128, STRIP, BLOCK), F32),
        ),
        in_specs=[smem, vmem],
        out_specs=(vmem, vmem),
        scratch_shapes=[pltpu.VMEM((SKY + 2, STRIP, BLOCK), F32)] * 3,
        compiler_params=pltpu.CompilerParams(vmem_limit_bytes=40 * 1024 * 1024),
    )(blocks, arrived)
    other = lax.ppermute(sends, "visit", [(i, i ^ 1) for i in range(8)])
    both = (keeps + other.astype(F32)).astype(BF16).reshape(TILES, 8, STRIP, BLOCK)
    parts = lax.all_to_all(both, "tile", split_axis=0, concat_axis=0, tiled=True)
    return pl.pallas_call(
        gather,
        out_shape=jax.ShapeDtypeStruct((32, 16 * BLOCK), F32),
        in_specs=[vmem],
        out_specs=vmem,
        compiler_params=pltpu.CompilerParams(vmem_limit_bytes=16 * 1024 * 1024),
    )(parts)


def solution(mesh):
    placed = (
        P("visit", "tile", None, None),
        P("visit", "tile"),
        P("visit", "tile", None),
        P(),
        P(),
        P("visit", None),
        P(),
    )
    return jax.shard_map(
        on_device, mesh=mesh, in_specs=placed, out_specs=P("visit", "tile"), check_vma=False
    )
```

```python
import functools

import jax
import jax.numpy as jnp
import numpy as np
from jax import lax
from jax.experimental import pallas as pl
from jax.experimental.pallas import tpu as pltpu
from jax.sharding import PartitionSpec as P

BLOCK = 128
TAPS = 31
HALF = 15
NBASIS = 9
PHASES = 16
PIECES = 14
H = 256
TILES = 16
STRIP = 16
STRIDE = 164
REACH = 18
COLS = 18 * BLOCK
META = PIECES * STRIDE
PAIRS = COLS // (2 * BLOCK)
FETCH = 7
AHEAD = 6
NEED = 144
DEPTH = NBASIS * NEED
SKY = 256
F32 = jnp.float32
BF16 = jnp.bfloat16


def tap_table():
    fraction = np.arange(PHASES)[:, None] / PHASES
    distance = np.arange(-3, 4)[None, :] - fraction
    raw = np.sinc(distance) * np.sinc(distance / 4.0)
    return raw / raw.sum(1, keepdims=True)


def bases():
    table = np.zeros((2 * PHASES, 3 * BLOCK), np.float32)
    taps = tap_table()
    for tap in range(7):
        table[:PHASES, (tap - 3) % BLOCK] = taps[:, tap]
        table[PHASES:, 6 - tap] = taps[:, tap]
    return table


def contribute(
    phase_in, dest_in, coef_in, vw_in, tab_in, brow_in, bcol_in, pix_in, out,
    phase, dest, coef, vw, tab, brow, bcol, pix, call, rall, xbuf, zbuf, sems, pix_sems,
):
    small = [
        pltpu.make_async_copy(source, target, sems.at[n])
        for n, (source, target) in enumerate(
            [
                (brow_in, brow), (bcol_in, bcol), (coef_in, coef), (vw_in, vw),
                (phase_in, phase), (tab_in, tab), (dest_in, dest),
            ]
        )
    ]
    for copy in small:
        copy.start()
    fetches = [
        pltpu.make_async_copy(pix_in.at[0, pl.ds(i, FETCH)], pix.at[pl.ds(i, FETCH)], pix_sems.at[i // FETCH])
        for i in range(0, PIECES, FETCH)
    ]
    for copy in fetches:
        copy.start()

    edge = lax.broadcasted_iota(jnp.int32, (8, BLOCK), 1)
    blank = jnp.zeros((BLOCK - 8, BLOCK), F32)
    lag = lax.broadcasted_iota(jnp.int32, (H, BLOCK), 0) - lax.broadcasted_iota(jnp.int32, (H, BLOCK), 1)
    inside = (lag >= 64 - HALF) & (lag <= 64 + HALF)

    def placing(base, width, step):
        tap = lax.broadcasted_iota(jnp.int32, (TAPS, width), 0)
        lane = lax.broadcasted_iota(jnp.int32, (TAPS, width), 1)
        at = base + step * tap
        at = jnp.where(at < 0, at + width, at)
        return jnp.where(lane == at, 1.0, 0.0).astype(BF16)

    for copy in small:
        copy.wait()
    visit = lax.axis_index("visit")
    total = vw[0]
    for other in range(1, 8):
        total = total + vw[other]
    share = jnp.full((1, BLOCK), vw[visit], F32) / jnp.full((1, BLOCK), total, F32)
    rowb = jnp.dot(brow[...], placing(-HALF, H, 1), preferred_element_type=F32)
    colb = jnp.dot(bcol[...], placing(HALF - 64, BLOCK, -1), preferred_element_type=F32)
    for k in range(NBASIS):
        line = colb[k : k + 1, :] * (share * coef[0, k])
        band = pltpu.roll(jnp.broadcast_to(line, (H, BLOCK)), 0, 1, stride=1, stride_axis=0)
        call[:, k * BLOCK : (k + 1) * BLOCK] = jnp.where(inside, band, 0.0).astype(BF16)
    for copy in fetches:
        copy.wait()
    written = set()
    talls = {}

    def lift(i):
        base = jnp.broadcast_to(tab[pl.ds(phase[0, i], 1), :][:, :BLOCK], (BLOCK, BLOCK))
        ring = pltpu.roll(base, 0, 1, stride=1, stride_axis=0)
        top, bottom = ring[:8], ring[120:]
        inner = jnp.concatenate(
            [jnp.where(edge >= 64, 0.0, top), ring[8:120], jnp.where(edge < 64, 0.0, bottom)], 0
        ).astype(BF16)
        beyond = jnp.concatenate([blank, jnp.where(edge < 64, bottom, 0.0)], 0).astype(BF16)
        before = jnp.concatenate([jnp.where(edge >= 64, top, 0.0), blank], 0).astype(BF16)
        row_op = jnp.concatenate(
            [jnp.concatenate([inner, beyond], 1), jnp.concatenate([before, inner], 1)], 0
        )
        talls[i] = jnp.dot(row_op, pix[i], preferred_element_type=F32).astype(BF16)

    def warp(i):
        if i + AHEAD < PIECES:
            lift(i + AHEAD)
        tall = talls.pop(i)
        block, offset = divmod(STRIDE * i + HALF + 64, BLOCK)
        count = -(-(offset + BLOCK + 6) // BLOCK)
        base = jnp.broadcast_to(tab[pl.ds(PHASES + phase[1, i], 1), :][:, : count * BLOCK], (8, count * BLOCK))
        base = jnp.broadcast_to(pltpu.roll(base, offset, 1)[:1], (BLOCK, count * BLOCK))
        col_op = pltpu.roll(base, 0, 1, stride=1, stride_axis=0).astype(BF16)
        window = jnp.dot(tall, col_op, preferred_element_type=F32).astype(BF16)
        for n in range(count):
            span = slice((block + n) * BLOCK, (block + n + 1) * BLOCK)
            part = window[:, n * BLOCK : (n + 1) * BLOCK]
            xbuf[:, span] = xbuf[:, span] + part if block + n in written else part
            written.add(block + n)

    def columns(p):
        for side in range(2):
            at = (2 * p + side) * BLOCK
            z = jnp.dot(xbuf[:, at : at + 2 * BLOCK], call[...], preferred_element_type=F32).astype(BF16)
            for k in range(NBASIS):
                zk = z[:, k * BLOCK : (k + 1) * BLOCK]
                for h in range(2):
                    at = DEPTH * h + NEED * k
                    zbuf[p % 2, at : at + NEED, side * BLOCK : (side + 1) * BLOCK] = zk[112 * h : 112 * h + NEED]

    def rows(p):
        got = [
            jnp.dot(
                rall[h, :, :DEPTH], zbuf[p % 2, DEPTH * h : DEPTH * (h + 1)], preferred_element_type=F32
            )
            for h in range(2)
        ]
        for strip in range(TILES):
            z, x = divmod(strip, 4)
            first = 64 * (z % 2) + 8 * x
            halves = [got[z // 2][first + 32 * c : first + 32 * c + 8] for c in range(2)]
            both = jnp.concatenate(halves, 0)
            if p == PAIRS - 1:
                row = lax.broadcasted_iota(jnp.int32, (STRIP, 2 * BLOCK), 0)
                lane = lax.broadcasted_iota(jnp.int32, (STRIP, 2 * BLOCK), 1)
                mark = jnp.zeros((STRIP, 2 * BLOCK), F32)
                for i in range(PIECES):
                    mark = jnp.where(row == i, dest[0, i].astype(F32), mark)
                both = jnp.where(lane >= META % (2 * BLOCK), mark, both)
            out[strip, :, 2 * p * BLOCK : 2 * (p + 1) * BLOCK] = both.astype(BF16)

    def rbuild():
        lane = lax.broadcasted_iota(jnp.int32, (BLOCK, H), 1)
        for h in range(2):
            for k in range(NBASIS):
                block, offset = divmod(NEED * k, BLOCK)
                base = jnp.broadcast_to(rowb[k : k + 1, :], (8, H))
                base = pltpu.roll(base, offset + STRIP * h, 1)
                band = pltpu.roll(jnp.broadcast_to(base[:1], (BLOCK, H)), 0, 1, stride=1, stride_axis=0)
                band = jnp.where((lane >= offset) & (lane < offset + NEED), band, 0.0).astype(BF16)
                for n in range(2):
                    span = slice((block + n) * BLOCK, (block + n + 1) * BLOCK)
                    part = band[:, n * BLOCK : (n + 1) * BLOCK]
                    rall[h, :, span] = rall[h, :, span] + part if n == 0 and offset else part

    def ready(p):
        while len(warped) < PIECES and STRIDE * len(warped) + HALF + 64 < (2 * p + 3) * BLOCK:
            warp(len(warped))
            warped.append(True)

    warped = []
    for i in range(AHEAD):
        lift(i)
    ready(0)
    for p in range(PAIRS + 1):
        if p < PAIRS:
            columns(p)
        if p == 0:
            rbuild()
        if p + 1 < PAIRS:
            ready(p + 1)
        if p > 0:
            rows(p - 1)


def place(goes, dest, arr, out, main, left, right):
    upper = lax.rem(lax.axis_index("visit"), 2) == (0 if goes else 1)
    for buf in (main, left, right):
        buf[...] = jnp.zeros_like(buf)
    lane = lax.broadcasted_iota(jnp.int32, (8, BLOCK), 1)
    for s in range(TILES):
        z = s // 4
        for i in range(PIECES):
            q, o = divmod(STRIDE * i + REACH, BLOCK)

            def turned(b):
                block = arr[s, :, b * BLOCK : (b + 1) * BLOCK].astype(F32)
                return pltpu.roll(jnp.where(upper, block[8:], block[:8]), (BLOCK - o) % BLOCK, 1)

            first, second = turned(q), turned(q + 1)
            body = jnp.where(lane < BLOCK - o, first, second)
            low = first
            if o < REACH:
                low = jnp.where(lane < BLOCK - o, turned(q - 1), first)
            low = jnp.where(lane >= BLOCK - REACH, low, 0.0)
            high = second
            if o + REACH > BLOCK:
                high = jnp.where(lane < BLOCK - o, second, turned(q + 2))
            high = jnp.where(lane < REACH, high, 0.0)
            d = dest[s, i]
            for buf, at, part in ((main, d + 1, body), (left, d, low), (right, d + 2, high)):
                buf[at] = part if z == 0 else buf[at] + part

    def fill(j, carry):
        for u in range(4):
            pair = j * 4 + u
            sides = []
            for side in range(2):
                at = 2 * pair + side + 1
                sides.append(main[at] + left[at] + right[at])
            out[pair] = jnp.concatenate(sides, 0).astype(out.dtype)
        return carry

    lax.fori_loop(0, SKY // 8, fill, 0, unroll=2)


def gather(arr, out):
    for x in range(4):
        for u in range(8):
            terms = [arr[4 * y + x, u].astype(F32) for y in range(4)]
            total = (terms[0] + terms[1]) + (terms[2] + terms[3])
            for side in range(2):
                at = (2 * u + side) * BLOCK
                out[8 * x : 8 * x + 8, at : at + BLOCK] = total[8 * side : 8 * side + 8]


def on_device(pixels, dest_block, phase_index, basis_row, basis_col, coefficients, visit_weight):
    smem = pl.BlockSpec(memory_space=pltpu.SMEM)
    vmem = pl.BlockSpec(memory_space=pltpu.VMEM)
    sent = pl.pallas_call(
        contribute,
        out_shape=jax.ShapeDtypeStruct((TILES, STRIP, COLS), BF16),
        in_specs=[pl.BlockSpec(memory_space=pltpu.HBM)] * 8,
        out_specs=vmem,
        scratch_shapes=[
            pltpu.SMEM((2, PIECES), jnp.int32),
            pltpu.SMEM((1, PIECES), jnp.int32),
            pltpu.SMEM((1, NBASIS), F32),
            pltpu.SMEM((8,), F32),
            pltpu.VMEM((2 * PHASES, 3 * BLOCK), F32),
            pltpu.VMEM((NBASIS, TAPS), BF16),
            pltpu.VMEM((NBASIS, TAPS), BF16),
            pltpu.VMEM((PIECES, H, BLOCK), BF16),
            pltpu.VMEM((H, NBASIS * BLOCK), BF16),
            pltpu.VMEM((2, BLOCK, 11 * BLOCK), BF16),
            pltpu.VMEM((H, COLS + BLOCK), BF16),
            pltpu.VMEM((2, 2 * DEPTH, 2 * BLOCK), BF16),
            pltpu.SemaphoreType.DMA((7,)),
            pltpu.SemaphoreType.DMA((PIECES // FETCH,)),
        ],
        compiler_params=pltpu.CompilerParams(vmem_limit_bytes=60 * 1024 * 1024),
    )(
        phase_index[0].T, dest_block, coefficients, visit_weight,
        jnp.asarray(bases()), basis_row, basis_col, pixels,
    )
    groups = [
        [(4 * y + x) * 8 + 2 * z + c for z in range(4) for x in range(4)]
        for c in range(2) for y in range(4)
    ]
    arrived = lax.all_to_all(
        sent, ("tile", "visit"), split_axis=0, concat_axis=0, tiled=True, axis_index_groups=groups
    )
    blocks = arrived[:, :PIECES, META].astype(jnp.int32)

    def placed(goes):
        return pl.pallas_call(
            functools.partial(place, goes),
            out_shape=jax.ShapeDtypeStruct((SKY // 2, STRIP, BLOCK), BF16 if goes else F32),
            in_specs=[smem, vmem],
            out_specs=vmem,
            scratch_shapes=[pltpu.VMEM((SKY + 2, 8, BLOCK), F32)] * 3,
            compiler_params=pltpu.CompilerParams(vmem_limit_bytes=40 * 1024 * 1024),
            cost_estimate=pl.CostEstimate(flops=10**7, bytes_accessed=4 * 10**6, transcendentals=0),
        )(blocks, arrived)

    sends, keeps = placed(True), placed(False)
    other = lax.ppermute(sends, "visit", [(i, i ^ 1) for i in range(8)])
    both = (keeps + other.astype(F32)).astype(BF16).reshape(TILES, 8, STRIP, BLOCK)
    parts = lax.all_to_all(both, "tile", split_axis=0, concat_axis=0, tiled=True)
    return pl.pallas_call(
        gather,
        out_shape=jax.ShapeDtypeStruct((32, 16 * BLOCK), F32),
        in_specs=[vmem],
        out_specs=vmem,
        compiler_params=pltpu.CompilerParams(vmem_limit_bytes=16 * 1024 * 1024),
    )(parts)


def solution(mesh):
    placed = (
        P("visit", "tile", None, None),
        P("visit", "tile"),
        P("visit", "tile", None),
        P(),
        P(),
        P("visit", None),
        P(),
    )
    return jax.shard_map(
        on_device, mesh=mesh, in_specs=placed, out_specs=P("visit", "tile"), check_vma=False
    )
```

```python
import functools

import jax
import jax.numpy as jnp
import numpy as np
from jax import lax
from jax.experimental import pallas as pl
from jax.experimental.pallas import tpu as pltpu
from jax.sharding import PartitionSpec as P

BLOCK = 128
TAPS = 31
HALF = 15
NBASIS = 9
PHASES = 16
PIECES = 14
H = 256
TILES = 16
STRIP = 16
STRIDE = 164
REACH = 18
COLS = 18 * BLOCK
META = PIECES * STRIDE
PAIRS = COLS // (2 * BLOCK)
FETCH = 7
AHEAD = 6
NEED = 144
DEPTH = NBASIS * NEED
SKY = 256
F32 = jnp.float32
BF16 = jnp.bfloat16


def tap_table():
    fraction = np.arange(PHASES)[:, None] / PHASES
    distance = np.arange(-3, 4)[None, :] - fraction
    raw = np.sinc(distance) * np.sinc(distance / 4.0)
    return raw / raw.sum(1, keepdims=True)


def bases():
    table = np.zeros((2 * PHASES, 3 * BLOCK), np.float32)
    taps = tap_table()
    for tap in range(7):
        table[:PHASES, (tap - 3) % BLOCK] = taps[:, tap]
        table[PHASES:, 6 - tap] = taps[:, tap]
    return table


def contribute(
    phase_in, dest_in, coef_in, vw_in, tab_in, brow_in, bcol_in, pix_in, out,
    phase, dest, coef, vw, tab, brow, bcol, pix, call, rall, xbuf, zbuf, sems, pix_sems,
):
    small = [
        pltpu.make_async_copy(source, target, sems.at[n])
        for n, (source, target) in enumerate(
            [
                (brow_in, brow), (bcol_in, bcol), (coef_in, coef), (vw_in, vw),
                (phase_in, phase), (tab_in, tab), (dest_in, dest),
            ]
        )
    ]
    for copy in small:
        copy.start()
    fetches = [
        pltpu.make_async_copy(pix_in.at[0, pl.ds(i, FETCH)], pix.at[pl.ds(i, FETCH)], pix_sems.at[i // FETCH])
        for i in range(0, PIECES, FETCH)
    ]
    for copy in fetches:
        copy.start()

    edge = lax.broadcasted_iota(jnp.int32, (8, BLOCK), 1)
    blank = jnp.zeros((BLOCK - 8, BLOCK), F32)
    lag = lax.broadcasted_iota(jnp.int32, (H, BLOCK), 0) - lax.broadcasted_iota(jnp.int32, (H, BLOCK), 1)
    inside = (lag >= 64 - HALF) & (lag <= 64 + HALF)

    def placing(base, width, step):
        tap = lax.broadcasted_iota(jnp.int32, (TAPS, width), 0)
        lane = lax.broadcasted_iota(jnp.int32, (TAPS, width), 1)
        at = base + step * tap
        at = jnp.where(at < 0, at + width, at)
        return jnp.where(lane == at, 1.0, 0.0).astype(BF16)

    for copy in small:
        copy.wait()
    visit = lax.axis_index("visit")
    total = vw[0]
    for other in range(1, 8):
        total = total + vw[other]
    share = jnp.full((1, BLOCK), vw[visit], F32) / jnp.full((1, BLOCK), total, F32)
    rowb = jnp.dot(brow[...], placing(-HALF, H, 1), preferred_element_type=F32)
    colb = jnp.dot(bcol[...], placing(HALF - 64, BLOCK, -1), preferred_element_type=F32)
    for k in range(NBASIS):
        line = colb[k : k + 1, :] * (share * coef[0, k])
        band = pltpu.roll(jnp.broadcast_to(line, (H, BLOCK)), 0, 1, stride=1, stride_axis=0)
        call[:, k * BLOCK : (k + 1) * BLOCK] = jnp.where(inside, band, 0.0).astype(BF16)
    for copy in fetches:
        copy.wait()
    written = set()
    talls = {}

    def lift(i):
        base = jnp.broadcast_to(tab[pl.ds(phase[0, i], 1), :][:, :BLOCK], (BLOCK, BLOCK))
        ring = pltpu.roll(base, 0, 1, stride=1, stride_axis=0)
        top, bottom = ring[:8], ring[120:]
        inner = jnp.concatenate(
            [jnp.where(edge >= 64, 0.0, top), ring[8:120], jnp.where(edge < 64, 0.0, bottom)], 0
        ).astype(BF16)
        beyond = jnp.concatenate([blank, jnp.where(edge < 64, bottom, 0.0)], 0).astype(BF16)
        before = jnp.concatenate([jnp.where(edge >= 64, top, 0.0), blank], 0).astype(BF16)
        row_op = jnp.concatenate(
            [jnp.concatenate([inner, beyond], 1), jnp.concatenate([before, inner], 1)], 0
        )
        talls[i] = jnp.dot(row_op, pix[i], preferred_element_type=F32).astype(BF16)

    def warp(i):
        if i + AHEAD < PIECES:
            lift(i + AHEAD)
        tall = talls.pop(i)
        block, offset = divmod(STRIDE * i + HALF + 64, BLOCK)
        count = -(-(offset + BLOCK + 6) // BLOCK)
        base = jnp.broadcast_to(tab[pl.ds(PHASES + phase[1, i], 1), :][:, : count * BLOCK], (8, count * BLOCK))
        base = jnp.broadcast_to(pltpu.roll(base, offset, 1)[:1], (BLOCK, count * BLOCK))
        col_op = pltpu.roll(base, 0, 1, stride=1, stride_axis=0).astype(BF16)
        window = jnp.dot(tall, col_op, preferred_element_type=F32).astype(BF16)
        for n in range(count):
            span = slice((block + n) * BLOCK, (block + n + 1) * BLOCK)
            part = window[:, n * BLOCK : (n + 1) * BLOCK]
            xbuf[:, span] = xbuf[:, span] + part if block + n in written else part
            written.add(block + n)

    def columns(p):
        for side in range(2):
            at = (2 * p + side) * BLOCK
            z = jnp.dot(xbuf[:, at : at + 2 * BLOCK], call[...], preferred_element_type=F32).astype(BF16)
            for k in range(NBASIS):
                zk = z[:, k * BLOCK : (k + 1) * BLOCK]
                for h in range(2):
                    at = DEPTH * h + NEED * k
                    zbuf[p % 2, at : at + NEED, side * BLOCK : (side + 1) * BLOCK] = zk[112 * h : 112 * h + NEED]

    def rows(p):
        got = [
            jnp.dot(
                rall[h, :, :DEPTH], zbuf[p % 2, DEPTH * h : DEPTH * (h + 1)], preferred_element_type=F32
            )
            for h in range(2)
        ]
        for strip in range(TILES):
            z, x = divmod(strip, 4)
            first = 64 * (z % 2) + 8 * x
            halves = [got[z // 2][first + 32 * c : first + 32 * c + 8] for c in range(2)]
            both = jnp.concatenate(halves, 0)
            if p == PAIRS - 1:
                row = lax.broadcasted_iota(jnp.int32, (STRIP, 2 * BLOCK), 0)
                lane = lax.broadcasted_iota(jnp.int32, (STRIP, 2 * BLOCK), 1)
                mark = jnp.zeros((STRIP, 2 * BLOCK), F32)
                for i in range(PIECES):
                    here = (row == i // 8) & (lane == META % (2 * BLOCK) + i % 8)
                    mark = jnp.where(here, dest[0, i].astype(F32), mark)
                both = jnp.where(lane >= META % (2 * BLOCK), mark, both)
            out[strip, :, 2 * p * BLOCK : 2 * (p + 1) * BLOCK] = both.astype(BF16)

    def rbuild():
        lane = lax.broadcasted_iota(jnp.int32, (BLOCK, H), 1)
        for h in range(2):
            for k in range(NBASIS):
                block, offset = divmod(NEED * k, BLOCK)
                base = jnp.broadcast_to(rowb[k : k + 1, :], (8, H))
                base = pltpu.roll(base, offset + STRIP * h, 1)
                band = pltpu.roll(jnp.broadcast_to(base[:1], (BLOCK, H)), 0, 1, stride=1, stride_axis=0)
                band = jnp.where((lane >= offset) & (lane < offset + NEED), band, 0.0).astype(BF16)
                for n in range(2):
                    span = slice((block + n) * BLOCK, (block + n + 1) * BLOCK)
                    part = band[:, n * BLOCK : (n + 1) * BLOCK]
                    rall[h, :, span] = rall[h, :, span] + part if n == 0 and offset else part

    def ready(p):
        while len(warped) < PIECES and STRIDE * len(warped) + HALF + 64 < (2 * p + 3) * BLOCK:
            warp(len(warped))
            warped.append(True)

    warped = []
    for i in range(AHEAD):
        lift(i)
    ready(0)
    for p in range(PAIRS + 1):
        if p < PAIRS:
            columns(p)
        if p == 0:
            rbuild()
        if p + 1 < PAIRS:
            ready(p + 1)
        if p > 0:
            rows(p - 1)


def place(goes, arr, out, main, left, right, words, dest, sem):
    upper = lax.rem(lax.axis_index("visit"), 2) == (0 if goes else 1)
    row = lax.broadcasted_iota(jnp.int32, (TILES, BLOCK), 0)
    lane = lax.broadcasted_iota(jnp.int32, (TILES, BLOCK), 1)
    low = high = jnp.zeros((TILES, BLOCK), F32)
    for s in range(TILES):
        tile = arr[s, :, COLS - BLOCK :].astype(F32)
        low = jnp.where(row == s, jnp.broadcast_to(tile[0:1], (TILES, BLOCK)), low)
        high = jnp.where(row == s, jnp.broadcast_to(tile[1:2], (TILES, BLOCK)), high)
    both = jnp.where(lane >= BLOCK - 8, low, pltpu.roll(high, BLOCK - 8, 1))
    words[...] = jnp.where(lane >= BLOCK - 16, both, 0.0).astype(jnp.int32)
    copy = pltpu.make_async_copy(words, dest, sem)
    copy.start()
    for buf in (main, left, right):
        buf[...] = jnp.zeros_like(buf)
    copy.wait()
    lane = lax.broadcasted_iota(jnp.int32, (8, BLOCK), 1)
    for s in range(TILES):
        z = s // 4
        for i in range(PIECES):
            q, o = divmod(STRIDE * i + REACH, BLOCK)

            def turned(b):
                block = arr[s, :, b * BLOCK : (b + 1) * BLOCK].astype(F32)
                return pltpu.roll(jnp.where(upper, block[8:], block[:8]), (BLOCK - o) % BLOCK, 1)

            first, second = turned(q), turned(q + 1)
            body = jnp.where(lane < BLOCK - o, first, second)
            low = first
            if o < REACH:
                low = jnp.where(lane < BLOCK - o, turned(q - 1), first)
            low = jnp.where(lane >= BLOCK - REACH, low, 0.0)
            high = second
            if o + REACH > BLOCK:
                high = jnp.where(lane < BLOCK - o, second, turned(q + 2))
            high = jnp.where(lane < REACH, high, 0.0)
            d = dest[s, BLOCK - 8 + i if i < 8 else BLOCK - 24 + i]
            for buf, at, part in ((main, d + 1, body), (left, d, low), (right, d + 2, high)):
                buf[at] = part if z == 0 else buf[at] + part

    def fill(j, carry):
        for u in range(4):
            pair = j * 4 + u
            sides = []
            for side in range(2):
                at = 2 * pair + side + 1
                sides.append(main[at] + left[at] + right[at])
            out[pair] = jnp.concatenate(sides, 0).astype(out.dtype)
        return carry

    lax.fori_loop(0, SKY // 8, fill, 0, unroll=2)


def gather(arr, out):
    for x in range(4):
        for u in range(8):
            terms = [arr[4 * y + x, u].astype(F32) for y in range(4)]
            total = (terms[0] + terms[1]) + (terms[2] + terms[3])
            for side in range(2):
                at = (2 * u + side) * BLOCK
                out[8 * x : 8 * x + 8, at : at + BLOCK] = total[8 * side : 8 * side + 8]


def on_device(pixels, dest_block, phase_index, basis_row, basis_col, coefficients, visit_weight):
    vmem = pl.BlockSpec(memory_space=pltpu.VMEM)
    sent = pl.pallas_call(
        contribute,
        out_shape=jax.ShapeDtypeStruct((TILES, STRIP, COLS), BF16),
        in_specs=[pl.BlockSpec(memory_space=pltpu.HBM)] * 8,
        out_specs=vmem,
        scratch_shapes=[
            pltpu.SMEM((2, PIECES), jnp.int32),
            pltpu.SMEM((1, PIECES), jnp.int32),
            pltpu.SMEM((1, NBASIS), F32),
            pltpu.SMEM((8,), F32),
            pltpu.VMEM((2 * PHASES, 3 * BLOCK), F32),
            pltpu.VMEM((NBASIS, TAPS), BF16),
            pltpu.VMEM((NBASIS, TAPS), BF16),
            pltpu.VMEM((PIECES, H, BLOCK), BF16),
            pltpu.VMEM((H, NBASIS * BLOCK), BF16),
            pltpu.VMEM((2, BLOCK, 11 * BLOCK), BF16),
            pltpu.VMEM((H, COLS + BLOCK), BF16),
            pltpu.VMEM((2, 2 * DEPTH, 2 * BLOCK), BF16),
            pltpu.SemaphoreType.DMA((7,)),
            pltpu.SemaphoreType.DMA((PIECES // FETCH,)),
        ],
        compiler_params=pltpu.CompilerParams(vmem_limit_bytes=60 * 1024 * 1024),
    )(
        phase_index[0].T, dest_block, coefficients, visit_weight,
        jnp.asarray(bases()), basis_row, basis_col, pixels,
    )
    groups = [
        [(4 * y + x) * 8 + 2 * z + c for z in range(4) for x in range(4)]
        for c in range(2) for y in range(4)
    ]
    arrived = lax.all_to_all(
        sent, ("tile", "visit"), split_axis=0, concat_axis=0, tiled=True, axis_index_groups=groups
    )

    def placed(goes):
        return pl.pallas_call(
            functools.partial(place, goes),
            out_shape=jax.ShapeDtypeStruct((SKY // 2, STRIP, BLOCK), BF16 if goes else F32),
            in_specs=[vmem],
            out_specs=vmem,
            scratch_shapes=[pltpu.VMEM((SKY + 2, 8, BLOCK), F32)] * 3
            + [
                pltpu.VMEM((TILES, BLOCK), jnp.int32),
                pltpu.SMEM((TILES, BLOCK), jnp.int32),
                pltpu.SemaphoreType.DMA,
            ],
            compiler_params=pltpu.CompilerParams(vmem_limit_bytes=40 * 1024 * 1024),
            cost_estimate=pl.CostEstimate(flops=10**7, bytes_accessed=4 * 10**6, transcendentals=0),
        )(arrived)

    sends, keeps = placed(True), placed(False)
    other = lax.ppermute(sends, "visit", [(i, i ^ 1) for i in range(8)])
    both = (keeps + other.astype(F32)).astype(BF16).reshape(TILES, 8, STRIP, BLOCK)
    parts = lax.all_to_all(both, "tile", split_axis=0, concat_axis=0, tiled=True)
    return pl.pallas_call(
        gather,
        out_shape=jax.ShapeDtypeStruct((32, 16 * BLOCK), F32),
        in_specs=[vmem],
        out_specs=vmem,
        compiler_params=pltpu.CompilerParams(vmem_limit_bytes=16 * 1024 * 1024),
    )(parts)


def solution(mesh):
    placed = (
        P("visit", "tile", None, None),
        P("visit", "tile"),
        P("visit", "tile", None),
        P(),
        P(),
        P("visit", None),
        P(),
    )
    return jax.shard_map(
        on_device, mesh=mesh, in_specs=placed, out_specs=P("visit", "tile"), check_vma=False
    )
```

```python
import functools

import jax
import jax.numpy as jnp
import numpy as np
from jax import lax
from jax.experimental import pallas as pl
from jax.experimental.pallas import tpu as pltpu
from jax.sharding import PartitionSpec as P

BLOCK = 128
TAPS = 31
HALF = 15
NBASIS = 9
PHASES = 16
PIECES = 14
H = 256
TILES = 16
STRIP = 16
STRIDE = 164
REACH = 18
COLS = 18 * BLOCK
META = PIECES * STRIDE
PAIRS = COLS // (2 * BLOCK)
FETCH = 7
AHEAD = 6
NEED = 144
DEPTH = NBASIS * NEED
SKY = 256
F32 = jnp.float32
BF16 = jnp.bfloat16


def tap_table():
    fraction = np.arange(PHASES)[:, None] / PHASES
    distance = np.arange(-3, 4)[None, :] - fraction
    raw = np.sinc(distance) * np.sinc(distance / 4.0)
    return raw / raw.sum(1, keepdims=True)


def bases():
    table = np.zeros((2 * PHASES, 3 * BLOCK), np.float32)
    taps = tap_table()
    for tap in range(7):
        table[:PHASES, (tap - 3) % BLOCK] = taps[:, tap]
        table[PHASES:, 6 - tap] = taps[:, tap]
    return table


def contribute(
    phase_in, dest_in, coef_in, vw_in, tab_in, brow_in, bcol_in, pix_in, out,
    phase, dest, coef, vw, tab, brow, bcol, pix, call, rall, xbuf, zbuf, sems, pix_sems,
):
    small = [
        pltpu.make_async_copy(source, target, sems.at[n])
        for n, (source, target) in enumerate(
            [
                (brow_in, brow), (bcol_in, bcol), (coef_in, coef), (vw_in, vw),
                (phase_in, phase), (tab_in, tab), (dest_in, dest),
            ]
        )
    ]
    for copy in small:
        copy.start()
    fetches = [
        pltpu.make_async_copy(pix_in.at[0, pl.ds(i, FETCH)], pix.at[pl.ds(i, FETCH)], pix_sems.at[i // FETCH])
        for i in range(0, PIECES, FETCH)
    ]
    for copy in fetches:
        copy.start()

    edge = lax.broadcasted_iota(jnp.int32, (8, BLOCK), 1)
    blank = jnp.zeros((BLOCK - 8, BLOCK), F32)
    lag = lax.broadcasted_iota(jnp.int32, (H, BLOCK), 0) - lax.broadcasted_iota(jnp.int32, (H, BLOCK), 1)
    inside = (lag >= 64 - HALF) & (lag <= 64 + HALF)

    def placing(base, width, step):
        tap = lax.broadcasted_iota(jnp.int32, (TAPS, width), 0)
        lane = lax.broadcasted_iota(jnp.int32, (TAPS, width), 1)
        at = base + step * tap
        at = jnp.where(at < 0, at + width, at)
        return jnp.where(lane == at, 1.0, 0.0).astype(BF16)

    for copy in small:
        copy.wait()
    visit = lax.axis_index("visit")
    total = vw[0]
    for other in range(1, 8):
        total = total + vw[other]
    share = jnp.full((1, BLOCK), vw[visit], F32) / jnp.full((1, BLOCK), total, F32)
    rowb = jnp.dot(brow[...], placing(-HALF, H, 1), preferred_element_type=F32)
    colb = jnp.dot(bcol[...], placing(HALF - 64, BLOCK, -1), preferred_element_type=F32)
    for k in range(NBASIS):
        line = colb[k : k + 1, :] * (share * coef[0, k])
        band = pltpu.roll(jnp.broadcast_to(line, (H, BLOCK)), 0, 1, stride=1, stride_axis=0)
        call[:, k * BLOCK : (k + 1) * BLOCK] = jnp.where(inside, band, 0.0).astype(BF16)
    for copy in fetches:
        copy.wait()
    written = set()
    talls = {}

    def lift(i):
        base = jnp.broadcast_to(tab[pl.ds(phase[0, i], 1), :][:, :BLOCK], (BLOCK, BLOCK))
        ring = pltpu.roll(base, 0, 1, stride=1, stride_axis=0)
        top, bottom = ring[:8], ring[120:]
        inner = jnp.concatenate(
            [jnp.where(edge >= 64, 0.0, top), ring[8:120], jnp.where(edge < 64, 0.0, bottom)], 0
        ).astype(BF16)
        beyond = jnp.concatenate([blank, jnp.where(edge < 64, bottom, 0.0)], 0).astype(BF16)
        before = jnp.concatenate([jnp.where(edge >= 64, top, 0.0), blank], 0).astype(BF16)
        row_op = jnp.concatenate(
            [jnp.concatenate([inner, beyond], 1), jnp.concatenate([before, inner], 1)], 0
        )
        talls[i] = jnp.dot(row_op, pix[i], preferred_element_type=F32).astype(BF16)

    def warp(i):
        if i + AHEAD < PIECES:
            lift(i + AHEAD)
        tall = talls.pop(i)
        block, offset = divmod(STRIDE * i + HALF + 64, BLOCK)
        count = -(-(offset + BLOCK + 6) // BLOCK)
        base = jnp.broadcast_to(tab[pl.ds(PHASES + phase[1, i], 1), :][:, : count * BLOCK], (8, count * BLOCK))
        base = jnp.broadcast_to(pltpu.roll(base, offset, 1)[:1], (BLOCK, count * BLOCK))
        col_op = pltpu.roll(base, 0, 1, stride=1, stride_axis=0).astype(BF16)
        window = jnp.dot(tall, col_op, preferred_element_type=F32).astype(BF16)
        for n in range(count):
            span = slice((block + n) * BLOCK, (block + n + 1) * BLOCK)
            part = window[:, n * BLOCK : (n + 1) * BLOCK]
            xbuf[:, span] = xbuf[:, span] + part if block + n in written else part
            written.add(block + n)

    def columns(p):
        for side in range(2):
            at = (2 * p + side) * BLOCK
            z = jnp.dot(xbuf[:, at : at + 2 * BLOCK], call[...], preferred_element_type=F32).astype(BF16)
            for k in range(NBASIS):
                zk = z[:, k * BLOCK : (k + 1) * BLOCK]
                for h in range(2):
                    at = DEPTH * h + NEED * k
                    zbuf[p % 2, at : at + NEED, side * BLOCK : (side + 1) * BLOCK] = zk[112 * h : 112 * h + NEED]

    def rows(p):
        got = [
            jnp.dot(
                rall[h, :, :DEPTH], zbuf[p % 2, DEPTH * h : DEPTH * (h + 1)], preferred_element_type=F32
            )
            for h in range(2)
        ]
        for strip in range(TILES):
            z, x = divmod(strip, 4)
            first = 64 * (z % 2) + 8 * x
            halves = [got[z // 2][first + 32 * c : first + 32 * c + 8] for c in range(2)]
            both = jnp.concatenate(halves, 0)
            if p == PAIRS - 1:
                row = lax.broadcasted_iota(jnp.int32, (STRIP, 2 * BLOCK), 0)
                lane = lax.broadcasted_iota(jnp.int32, (STRIP, 2 * BLOCK), 1)
                mark = jnp.zeros((STRIP, 2 * BLOCK), F32)
                for i in range(PIECES):
                    here = (row == i // 8) & (lane == META % (2 * BLOCK) + i % 8)
                    mark = jnp.where(here, dest[0, i].astype(F32), mark)
                both = jnp.where(lane >= META % (2 * BLOCK), mark, both)
            out[strip, :, 2 * p * BLOCK : 2 * (p + 1) * BLOCK] = both.astype(BF16)

    def rbuild():
        lane = lax.broadcasted_iota(jnp.int32, (BLOCK, H), 1)
        for h in range(2):
            for k in range(NBASIS):
                block, offset = divmod(NEED * k, BLOCK)
                base = jnp.broadcast_to(rowb[k : k + 1, :], (8, H))
                base = pltpu.roll(base, offset + STRIP * h, 1)
                band = pltpu.roll(jnp.broadcast_to(base[:1], (BLOCK, H)), 0, 1, stride=1, stride_axis=0)
                band = jnp.where((lane >= offset) & (lane < offset + NEED), band, 0.0).astype(BF16)
                for n in range(2):
                    span = slice((block + n) * BLOCK, (block + n + 1) * BLOCK)
                    part = band[:, n * BLOCK : (n + 1) * BLOCK]
                    rall[h, :, span] = rall[h, :, span] + part if n == 0 and offset else part

    def ready(p):
        while len(warped) < PIECES and STRIDE * len(warped) + HALF + 64 < (2 * p + 3) * BLOCK:
            warp(len(warped))
            warped.append(True)

    warped = []
    for i in range(AHEAD):
        lift(i)
    ready(0)
    for p in range(PAIRS + 1):
        if p < PAIRS:
            columns(p)
        if p == 0:
            rbuild()
        if p + 1 < PAIRS:
            ready(p + 1)
        if p > 0:
            rows(p - 1)


def place(goes, arr, out, main, left, right, words, dest, sem):
    upper = lax.rem(lax.axis_index("visit"), 2) == (0 if goes else 1)
    row = lax.broadcasted_iota(jnp.int32, (TILES, BLOCK), 0)
    lane = lax.broadcasted_iota(jnp.int32, (TILES, BLOCK), 1)
    low = high = jnp.zeros((TILES, BLOCK), F32)
    for s in range(TILES):
        tile = arr[s, :, COLS - BLOCK :].astype(F32)
        low = jnp.where(row == s, jnp.broadcast_to(tile[0:1], (TILES, BLOCK)), low)
        high = jnp.where(row == s, jnp.broadcast_to(tile[1:2], (TILES, BLOCK)), high)
    both = jnp.where(lane >= BLOCK - 8, low, pltpu.roll(high, BLOCK - 8, 1))
    words[...] = jnp.where(lane >= BLOCK - 16, both, 0.0).astype(jnp.int32)
    copy = pltpu.make_async_copy(words, dest, sem)
    copy.start()
    for buf in (main, left, right):
        buf[...] = jnp.zeros_like(buf)
    copy.wait()
    lane = lax.broadcasted_iota(jnp.int32, (8, BLOCK), 1)
    for s in range(TILES):
        z = s // 4
        for i in range(PIECES):
            q, o = divmod(STRIDE * i + REACH, BLOCK)

            def turned(b):
                block = arr[s, :, b * BLOCK : (b + 1) * BLOCK].astype(F32)
                return pltpu.roll(jnp.where(upper, block[8:], block[:8]), (BLOCK - o) % BLOCK, 1)

            first, second = turned(q), turned(q + 1)
            body = jnp.where(lane < BLOCK - o, first, second)
            low = first
            if o < REACH:
                low = jnp.where(lane < BLOCK - o, turned(q - 1), first)
            low = jnp.where(lane >= BLOCK - REACH, low, 0.0)
            high = second
            if o + REACH > BLOCK:
                high = jnp.where(lane < BLOCK - o, second, turned(q + 2))
            high = jnp.where(lane < REACH, high, 0.0)
            d = dest[s, BLOCK - 8 + i if i < 8 else BLOCK - 24 + i]
            for buf, at, part in ((main, d + 1, body), (left, d, low), (right, d + 2, high)):
                buf[at] = part if z == 0 else buf[at] + part

    def fill(j, carry):
        for u in range(4):
            pair = j * 4 + u
            sides = []
            for side in range(2):
                at = 2 * pair + side + 1
                sides.append(main[at] + left[at] + right[at])
            out[8 * (TILES - 1 - j // 2) + j % 2 * 4 + u] = jnp.concatenate(sides, 0).astype(out.dtype)
        return carry

    lax.fori_loop(0, SKY // 8, fill, 0, unroll=2)


def gather(arr, out):
    for x in range(4):
        for u in range(8):
            terms = [arr[TILES - 1 - 4 * y - x, u].astype(F32) for y in range(4)]
            total = (terms[0] + terms[1]) + (terms[2] + terms[3])
            for side in range(2):
                at = (2 * u + side) * BLOCK
                out[8 * x : 8 * x + 8, at : at + BLOCK] = total[8 * side : 8 * side + 8]


def on_device(pixels, dest_block, phase_index, basis_row, basis_col, coefficients, visit_weight):
    vmem = pl.BlockSpec(memory_space=pltpu.VMEM)
    sent = pl.pallas_call(
        contribute,
        out_shape=jax.ShapeDtypeStruct((TILES, STRIP, COLS), BF16),
        in_specs=[pl.BlockSpec(memory_space=pltpu.HBM)] * 8,
        out_specs=vmem,
        scratch_shapes=[
            pltpu.SMEM((2, PIECES), jnp.int32),
            pltpu.SMEM((1, PIECES), jnp.int32),
            pltpu.SMEM((1, NBASIS), F32),
            pltpu.SMEM((8,), F32),
            pltpu.VMEM((2 * PHASES, 3 * BLOCK), F32),
            pltpu.VMEM((NBASIS, TAPS), BF16),
            pltpu.VMEM((NBASIS, TAPS), BF16),
            pltpu.VMEM((PIECES, H, BLOCK), BF16),
            pltpu.VMEM((H, NBASIS * BLOCK), BF16),
            pltpu.VMEM((2, BLOCK, 11 * BLOCK), BF16),
            pltpu.VMEM((H, COLS + BLOCK), BF16),
            pltpu.VMEM((2, 2 * DEPTH, 2 * BLOCK), BF16),
            pltpu.SemaphoreType.DMA((7,)),
            pltpu.SemaphoreType.DMA((PIECES // FETCH,)),
        ],
        compiler_params=pltpu.CompilerParams(vmem_limit_bytes=60 * 1024 * 1024),
    )(
        phase_index[0].T, dest_block, coefficients, visit_weight,
        jnp.asarray(bases()), basis_row, basis_col, pixels,
    )
    groups = [
        [(4 * y + x) * 8 + 2 * z + c for z in range(4) for x in range(4)]
        for c in range(2) for y in range(4)
    ]
    arrived = lax.all_to_all(
        sent, ("tile", "visit"), split_axis=0, concat_axis=0, tiled=True, axis_index_groups=groups
    )

    def placed(goes):
        return pl.pallas_call(
            functools.partial(place, goes),
            out_shape=jax.ShapeDtypeStruct((SKY // 2, STRIP, BLOCK), BF16 if goes else F32),
            in_specs=[vmem],
            out_specs=vmem,
            scratch_shapes=[pltpu.VMEM((SKY + 2, 8, BLOCK), F32)] * 3
            + [
                pltpu.VMEM((TILES, BLOCK), jnp.int32),
                pltpu.SMEM((TILES, BLOCK), jnp.int32),
                pltpu.SemaphoreType.DMA,
            ],
            compiler_params=pltpu.CompilerParams(vmem_limit_bytes=40 * 1024 * 1024),
            cost_estimate=pl.CostEstimate(flops=10**7, bytes_accessed=4 * 10**6, transcendentals=0),
        )(arrived)

    sends, keeps = placed(True), placed(False)
    other = lax.ppermute(sends, "visit", [(i, i ^ 1) for i in range(8)])
    both = (keeps + other.astype(F32)).astype(BF16).reshape(TILES, 8, STRIP, BLOCK)
    backward = [[8 * t + visit for t in reversed(range(TILES))] for visit in range(8)]
    parts = lax.all_to_all(
        both, ("tile", "visit"), split_axis=0, concat_axis=0, tiled=True, axis_index_groups=backward
    )
    return pl.pallas_call(
        gather,
        out_shape=jax.ShapeDtypeStruct((32, 16 * BLOCK), F32),
        in_specs=[vmem],
        out_specs=vmem,
        compiler_params=pltpu.CompilerParams(vmem_limit_bytes=16 * 1024 * 1024),
    )(parts)


def solution(mesh):
    placed = (
        P("visit", "tile", None, None),
        P("visit", "tile"),
        P("visit", "tile", None),
        P(),
        P(),
        P("visit", None),
        P(),
    )
    return jax.shard_map(
        on_device, mesh=mesh, in_specs=placed, out_specs=P("visit", "tile"), check_vma=False
    )
```

```python
import functools

import jax
import jax.numpy as jnp
import numpy as np
from jax import lax
from jax.experimental import pallas as pl
from jax.experimental.pallas import tpu as pltpu
from jax.sharding import PartitionSpec as P

BLOCK = 128
TAPS = 31
HALF = 15
NBASIS = 9
PHASES = 16
PIECES = 14
H = 256
TILES = 16
STRIP = 16
STRIDE = 164
REACH = 18
COLS = 18 * BLOCK
META = PIECES * STRIDE
PAIRS = COLS // (2 * BLOCK)
FETCH = 7
AHEAD = 6
NEED = 144
DEPTH = NBASIS * NEED
SKY = 256
F32 = jnp.float32
BF16 = jnp.bfloat16


def tap_table():
    fraction = np.arange(PHASES)[:, None] / PHASES
    distance = np.arange(-3, 4)[None, :] - fraction
    raw = np.sinc(distance) * np.sinc(distance / 4.0)
    return raw / raw.sum(1, keepdims=True)


def bases():
    table = np.zeros((2 * PHASES, 3 * BLOCK), np.float32)
    taps = tap_table()
    for tap in range(7):
        table[:PHASES, (tap - 3) % BLOCK] = taps[:, tap]
        table[PHASES:, 6 - tap] = taps[:, tap]
    return table


def contribute(
    phase_in, dest_in, coef_in, vw_in, tab_in, brow_in, bcol_in, pix_in, out,
    phase, dest, coef, vw, tab, brow, bcol, pix, call, rall, xbuf, zbuf, sems, pix_sems,
):
    small = [
        pltpu.make_async_copy(source, target, sems.at[n])
        for n, (source, target) in enumerate(
            [
                (brow_in, brow), (bcol_in, bcol), (coef_in, coef), (vw_in, vw),
                (phase_in, phase), (tab_in, tab), (dest_in, dest),
            ]
        )
    ]
    for copy in small:
        copy.start()
    fetches = [
        pltpu.make_async_copy(pix_in.at[0, pl.ds(i, FETCH)], pix.at[pl.ds(i, FETCH)], pix_sems.at[i // FETCH])
        for i in range(0, PIECES, FETCH)
    ]
    for copy in fetches:
        copy.start()

    edge = lax.broadcasted_iota(jnp.int32, (8, BLOCK), 1)
    blank = jnp.zeros((BLOCK - 8, BLOCK), F32)
    lag = lax.broadcasted_iota(jnp.int32, (H, BLOCK), 0) - lax.broadcasted_iota(jnp.int32, (H, BLOCK), 1)
    inside = (lag >= 64 - HALF) & (lag <= 64 + HALF)

    def placing(base, width, step):
        tap = lax.broadcasted_iota(jnp.int32, (TAPS, width), 0)
        lane = lax.broadcasted_iota(jnp.int32, (TAPS, width), 1)
        at = base + step * tap
        at = jnp.where(at < 0, at + width, at)
        return jnp.where(lane == at, 1.0, 0.0).astype(BF16)

    for copy in small:
        copy.wait()
    visit = lax.axis_index("visit")
    total = vw[0]
    for other in range(1, 8):
        total = total + vw[other]
    share = jnp.full((1, BLOCK), vw[visit], F32) / jnp.full((1, BLOCK), total, F32)
    rowb = jnp.dot(brow[...], placing(-HALF, H, 1), preferred_element_type=F32)
    colb = jnp.dot(bcol[...], placing(HALF - 64, BLOCK, -1), preferred_element_type=F32)
    for k in range(NBASIS):
        line = colb[k : k + 1, :] * (share * coef[0, k])
        band = pltpu.roll(jnp.broadcast_to(line, (H, BLOCK)), 0, 1, stride=1, stride_axis=0)
        call[:, k * BLOCK : (k + 1) * BLOCK] = jnp.where(inside, band, 0.0).astype(BF16)
    for copy in fetches:
        copy.wait()
    written = set()
    talls = {}

    def lift(i):
        base = jnp.broadcast_to(tab[pl.ds(phase[0, i], 1), :][:, :BLOCK], (BLOCK, BLOCK))
        ring = pltpu.roll(base, 0, 1, stride=1, stride_axis=0)
        top, bottom = ring[:8], ring[120:]
        inner = jnp.concatenate(
            [jnp.where(edge >= 64, 0.0, top), ring[8:120], jnp.where(edge < 64, 0.0, bottom)], 0
        ).astype(BF16)
        beyond = jnp.concatenate([blank, jnp.where(edge < 64, bottom, 0.0)], 0).astype(BF16)
        before = jnp.concatenate([jnp.where(edge >= 64, top, 0.0), blank], 0).astype(BF16)
        row_op = jnp.concatenate(
            [jnp.concatenate([inner, beyond], 1), jnp.concatenate([before, inner], 1)], 0
        )
        talls[i] = jnp.dot(row_op, pix[i], preferred_element_type=F32).astype(BF16)

    def warp(i):
        if i + AHEAD < PIECES:
            lift(i + AHEAD)
        tall = talls.pop(i)
        block, offset = divmod(STRIDE * i + HALF + 64, BLOCK)
        count = -(-(offset + BLOCK + 6) // BLOCK)
        base = jnp.broadcast_to(tab[pl.ds(PHASES + phase[1, i], 1), :][:, : count * BLOCK], (8, count * BLOCK))
        base = jnp.broadcast_to(pltpu.roll(base, offset, 1)[:1], (BLOCK, count * BLOCK))
        col_op = pltpu.roll(base, 0, 1, stride=1, stride_axis=0).astype(BF16)
        window = jnp.dot(tall, col_op, preferred_element_type=F32).astype(BF16)
        for n in range(count):
            span = slice((block + n) * BLOCK, (block + n + 1) * BLOCK)
            part = window[:, n * BLOCK : (n + 1) * BLOCK]
            xbuf[:, span] = xbuf[:, span] + part if block + n in written else part
            written.add(block + n)

    def columns(p):
        for side in range(2):
            at = (2 * p + side) * BLOCK
            z = jnp.dot(xbuf[:, at : at + 2 * BLOCK], call[...], preferred_element_type=F32).astype(BF16)
            for k in range(NBASIS):
                zk = z[:, k * BLOCK : (k + 1) * BLOCK]
                for h in range(2):
                    at = DEPTH * h + NEED * k
                    zbuf[p % 2, at : at + NEED, side * BLOCK : (side + 1) * BLOCK] = zk[112 * h : 112 * h + NEED]

    def rows(p):
        got = [
            jnp.dot(
                rall[h, :, :DEPTH], zbuf[p % 2, DEPTH * h : DEPTH * (h + 1)], preferred_element_type=F32
            )
            for h in range(2)
        ]
        for strip in range(TILES):
            z, x = divmod(strip, 4)
            first = 64 * (z % 2) + 8 * x
            halves = [got[z // 2][first + 32 * c : first + 32 * c + 8] for c in range(2)]
            both = jnp.concatenate(halves, 0)
            if p == PAIRS - 1:
                row = lax.broadcasted_iota(jnp.int32, (STRIP, 2 * BLOCK), 0)
                lane = lax.broadcasted_iota(jnp.int32, (STRIP, 2 * BLOCK), 1)
                mark = jnp.zeros((STRIP, 2 * BLOCK), F32)
                for i in range(PIECES):
                    here = (row == i // 8) & (lane == META % (2 * BLOCK) + i % 8)
                    mark = jnp.where(here, dest[0, i].astype(F32), mark)
                both = jnp.where(lane >= META % (2 * BLOCK), mark, both)
            out[TILES - 1 - strip, :, 2 * p * BLOCK : 2 * (p + 1) * BLOCK] = both.astype(BF16)

    def rbuild():
        lane = lax.broadcasted_iota(jnp.int32, (BLOCK, H), 1)
        for h in range(2):
            for k in range(NBASIS):
                block, offset = divmod(NEED * k, BLOCK)
                base = jnp.broadcast_to(rowb[k : k + 1, :], (8, H))
                base = pltpu.roll(base, offset + STRIP * h, 1)
                band = pltpu.roll(jnp.broadcast_to(base[:1], (BLOCK, H)), 0, 1, stride=1, stride_axis=0)
                band = jnp.where((lane >= offset) & (lane < offset + NEED), band, 0.0).astype(BF16)
                for n in range(2):
                    span = slice((block + n) * BLOCK, (block + n + 1) * BLOCK)
                    part = band[:, n * BLOCK : (n + 1) * BLOCK]
                    rall[h, :, span] = rall[h, :, span] + part if n == 0 and offset else part

    def ready(p):
        while len(warped) < PIECES and STRIDE * len(warped) + HALF + 64 < (2 * p + 3) * BLOCK:
            warp(len(warped))
            warped.append(True)

    warped = []
    for i in range(AHEAD):
        lift(i)
    ready(0)
    for p in range(PAIRS + 1):
        if p < PAIRS:
            columns(p)
        if p == 0:
            rbuild()
        if p + 1 < PAIRS:
            ready(p + 1)
        if p > 0:
            rows(p - 1)


def place(goes, arr, out, main, left, right, words, dest, sem):
    upper = lax.rem(lax.axis_index("visit"), 2) == (0 if goes else 1)
    row = lax.broadcasted_iota(jnp.int32, (TILES, BLOCK), 0)
    lane = lax.broadcasted_iota(jnp.int32, (TILES, BLOCK), 1)
    low = high = jnp.zeros((TILES, BLOCK), F32)
    for s in range(TILES):
        tile = arr[s, :, COLS - BLOCK :].astype(F32)
        low = jnp.where(row == s, jnp.broadcast_to(tile[0:1], (TILES, BLOCK)), low)
        high = jnp.where(row == s, jnp.broadcast_to(tile[1:2], (TILES, BLOCK)), high)
    both = jnp.where(lane >= BLOCK - 8, low, pltpu.roll(high, BLOCK - 8, 1))
    words[...] = jnp.where(lane >= BLOCK - 16, both, 0.0).astype(jnp.int32)
    copy = pltpu.make_async_copy(words, dest, sem)
    copy.start()
    for buf in (main, left, right):
        buf[...] = jnp.zeros_like(buf)
    copy.wait()
    lane = lax.broadcasted_iota(jnp.int32, (8, BLOCK), 1)
    for s in range(TILES):
        z = s // 4
        for i in range(PIECES):
            q, o = divmod(STRIDE * i + REACH, BLOCK)

            def turned(b):
                block = arr[s, :, b * BLOCK : (b + 1) * BLOCK].astype(F32)
                return pltpu.roll(jnp.where(upper, block[8:], block[:8]), (BLOCK - o) % BLOCK, 1)

            first, second = turned(q), turned(q + 1)
            body = jnp.where(lane < BLOCK - o, first, second)
            low = first
            if o < REACH:
                low = jnp.where(lane < BLOCK - o, turned(q - 1), first)
            low = jnp.where(lane >= BLOCK - REACH, low, 0.0)
            high = second
            if o + REACH > BLOCK:
                high = jnp.where(lane < BLOCK - o, second, turned(q + 2))
            high = jnp.where(lane < REACH, high, 0.0)
            d = dest[s, BLOCK - 8 + i if i < 8 else BLOCK - 24 + i]
            for buf, at, part in ((main, d + 1, body), (left, d, low), (right, d + 2, high)):
                buf[at] = part if z == 0 else buf[at] + part

    def fill(j, carry):
        for u in range(4):
            pair = j * 4 + u
            sides = []
            for side in range(2):
                at = 2 * pair + side + 1
                sides.append(main[at] + left[at] + right[at])
            out[8 * (TILES - 1 - j // 2) + j % 2 * 4 + u] = jnp.concatenate(sides, 0).astype(out.dtype)
        return carry

    lax.fori_loop(0, SKY // 8, fill, 0, unroll=2)


def gather(arr, out):
    for x in range(4):
        for u in range(8):
            terms = [arr[TILES - 1 - 4 * y - x, u].astype(F32) for y in range(4)]
            total = (terms[0] + terms[1]) + (terms[2] + terms[3])
            for side in range(2):
                at = (2 * u + side) * BLOCK
                out[8 * x : 8 * x + 8, at : at + BLOCK] = total[8 * side : 8 * side + 8]


def on_device(pixels, dest_block, phase_index, basis_row, basis_col, coefficients, visit_weight):
    vmem = pl.BlockSpec(memory_space=pltpu.VMEM)
    sent = pl.pallas_call(
        contribute,
        out_shape=jax.ShapeDtypeStruct((TILES, STRIP, COLS), BF16),
        in_specs=[pl.BlockSpec(memory_space=pltpu.HBM)] * 8,
        out_specs=vmem,
        scratch_shapes=[
            pltpu.SMEM((2, PIECES), jnp.int32),
            pltpu.SMEM((1, PIECES), jnp.int32),
            pltpu.SMEM((1, NBASIS), F32),
            pltpu.SMEM((8,), F32),
            pltpu.VMEM((2 * PHASES, 3 * BLOCK), F32),
            pltpu.VMEM((NBASIS, TAPS), BF16),
            pltpu.VMEM((NBASIS, TAPS), BF16),
            pltpu.VMEM((PIECES, H, BLOCK), BF16),
            pltpu.VMEM((H, NBASIS * BLOCK), BF16),
            pltpu.VMEM((2, BLOCK, 11 * BLOCK), BF16),
            pltpu.VMEM((H, COLS + BLOCK), BF16),
            pltpu.VMEM((2, 2 * DEPTH, 2 * BLOCK), BF16),
            pltpu.SemaphoreType.DMA((7,)),
            pltpu.SemaphoreType.DMA((PIECES // FETCH,)),
        ],
        compiler_params=pltpu.CompilerParams(vmem_limit_bytes=60 * 1024 * 1024),
    )(
        phase_index[0].T, dest_block, coefficients, visit_weight,
        jnp.asarray(bases()), basis_row, basis_col, pixels,
    )
    groups = [
        [(4 * y + x) * 8 + 2 * z + c for z in reversed(range(4)) for x in reversed(range(4))]
        for c in range(2) for y in range(4)
    ]
    arrived = lax.all_to_all(
        sent, ("tile", "visit"), split_axis=0, concat_axis=0, tiled=True, axis_index_groups=groups
    )

    def placed(goes):
        return pl.pallas_call(
            functools.partial(place, goes),
            out_shape=jax.ShapeDtypeStruct((SKY // 2, STRIP, BLOCK), BF16 if goes else F32),
            in_specs=[vmem],
            out_specs=vmem,
            scratch_shapes=[pltpu.VMEM((SKY + 2, 8, BLOCK), F32)] * 3
            + [
                pltpu.VMEM((TILES, BLOCK), jnp.int32),
                pltpu.SMEM((TILES, BLOCK), jnp.int32),
                pltpu.SemaphoreType.DMA,
            ],
            compiler_params=pltpu.CompilerParams(vmem_limit_bytes=40 * 1024 * 1024),
            cost_estimate=pl.CostEstimate(flops=10**7, bytes_accessed=4 * 10**6, transcendentals=0),
        )(arrived)

    sends, keeps = placed(True), placed(False)
    other = lax.ppermute(sends, "visit", [(i, i ^ 1) for i in range(8)])
    both = (keeps + other.astype(F32)).astype(BF16).reshape(TILES, 8, STRIP, BLOCK)
    backward = [[8 * t + visit for t in reversed(range(TILES))] for visit in range(8)]
    parts = lax.all_to_all(
        both, ("tile", "visit"), split_axis=0, concat_axis=0, tiled=True, axis_index_groups=backward
    )
    return pl.pallas_call(
        gather,
        out_shape=jax.ShapeDtypeStruct((32, 16 * BLOCK), F32),
        in_specs=[vmem],
        out_specs=vmem,
        compiler_params=pltpu.CompilerParams(vmem_limit_bytes=16 * 1024 * 1024),
    )(parts)


def solution(mesh):
    placed = (
        P("visit", "tile", None, None),
        P("visit", "tile"),
        P("visit", "tile", None),
        P(),
        P(),
        P("visit", None),
        P(),
    )
    return jax.shard_map(
        on_device, mesh=mesh, in_specs=placed, out_specs=P("visit", "tile"), check_vma=False
    )
```

```python
import functools

import jax
import jax.numpy as jnp
import numpy as np
from jax import lax
from jax.experimental import pallas as pl
from jax.experimental.pallas import tpu as pltpu
from jax.sharding import PartitionSpec as P

BLOCK = 128
TAPS = 31
HALF = 15
NBASIS = 9
PHASES = 16
PIECES = 14
H = 256
TILES = 16
STRIP = 16
STRIDE = 164
REACH = 18
COLS = 18 * BLOCK
META = PIECES * STRIDE
PAIRS = COLS // (2 * BLOCK)
FETCH = 7
AHEAD = 6
NEED = 144
DEPTH = NBASIS * NEED
SKY = 256
F32 = jnp.float32
BF16 = jnp.bfloat16


def tap_table():
    fraction = np.arange(PHASES)[:, None] / PHASES
    distance = np.arange(-3, 4)[None, :] - fraction
    raw = np.sinc(distance) * np.sinc(distance / 4.0)
    return raw / raw.sum(1, keepdims=True)


def bases():
    table = np.zeros((2 * PHASES, 3 * BLOCK), np.float32)
    taps = tap_table()
    for tap in range(7):
        table[:PHASES, (tap - 3) % BLOCK] = taps[:, tap]
        table[PHASES:, 6 - tap] = taps[:, tap]
    return table


def contribute(
    phase_in, dest_in, coef_in, vw_in, tab_in, brow_in, bcol_in, pix_in, out,
    phase, dest, coef, vw, tab, brow, bcol, pix, call, rall, xbuf, zbuf, sems, pix_sems,
):
    small = [
        pltpu.make_async_copy(source, target, sems.at[n])
        for n, (source, target) in enumerate(
            [
                (brow_in, brow), (bcol_in, bcol), (coef_in, coef), (vw_in, vw),
                (phase_in, phase), (tab_in, tab), (dest_in, dest),
            ]
        )
    ]
    for copy in small:
        copy.start()
    fetches = [
        pltpu.make_async_copy(pix_in.at[0, pl.ds(i, FETCH)], pix.at[pl.ds(i, FETCH)], pix_sems.at[i // FETCH])
        for i in range(0, PIECES, FETCH)
    ]
    for copy in fetches:
        copy.start()

    edge = lax.broadcasted_iota(jnp.int32, (8, BLOCK), 1)
    blank = jnp.zeros((BLOCK - 8, BLOCK), F32)
    lag = lax.broadcasted_iota(jnp.int32, (H, BLOCK), 0) - lax.broadcasted_iota(jnp.int32, (H, BLOCK), 1)
    inside = (lag >= 64 - HALF) & (lag <= 64 + HALF)

    def placing(base, width, step):
        tap = lax.broadcasted_iota(jnp.int32, (TAPS, width), 0)
        lane = lax.broadcasted_iota(jnp.int32, (TAPS, width), 1)
        at = base + step * tap
        at = jnp.where(at < 0, at + width, at)
        return jnp.where(lane == at, 1.0, 0.0).astype(BF16)

    for copy in small:
        copy.wait()
    visit = lax.axis_index("visit")
    total = vw[0]
    for other in range(1, 8):
        total = total + vw[other]
    share = jnp.full((1, BLOCK), vw[visit], F32) / jnp.full((1, BLOCK), total, F32)
    rowb = jnp.dot(brow[...], placing(-HALF, H, 1), preferred_element_type=F32)
    colb = jnp.dot(bcol[...], placing(HALF - 64, BLOCK, -1), preferred_element_type=F32)
    for k in range(NBASIS):
        line = colb[k : k + 1, :] * (share * coef[0, k])
        band = pltpu.roll(jnp.broadcast_to(line, (H, BLOCK)), 0, 1, stride=1, stride_axis=0)
        call[:, k * BLOCK : (k + 1) * BLOCK] = jnp.where(inside, band, 0.0).astype(BF16)
    for copy in fetches:
        copy.wait()
    written = set()
    talls = {}

    def lift(i):
        base = jnp.broadcast_to(tab[pl.ds(phase[0, i], 1), :][:, :BLOCK], (BLOCK, BLOCK))
        ring = pltpu.roll(base, 0, 1, stride=1, stride_axis=0)
        top, bottom = ring[:8], ring[120:]
        inner = jnp.concatenate(
            [jnp.where(edge >= 64, 0.0, top), ring[8:120], jnp.where(edge < 64, 0.0, bottom)], 0
        ).astype(BF16)
        beyond = jnp.concatenate([blank, jnp.where(edge < 64, bottom, 0.0)], 0).astype(BF16)
        before = jnp.concatenate([jnp.where(edge >= 64, top, 0.0), blank], 0).astype(BF16)
        row_op = jnp.concatenate(
            [jnp.concatenate([inner, beyond], 1), jnp.concatenate([before, inner], 1)], 0
        )
        talls[i] = jnp.dot(row_op, pix[i], preferred_element_type=F32).astype(BF16)

    def warp(i):
        if i + AHEAD < PIECES:
            lift(i + AHEAD)
        tall = talls.pop(i)
        block, offset = divmod(STRIDE * i + HALF + 64, BLOCK)
        count = -(-(offset + BLOCK + 6) // BLOCK)
        base = jnp.broadcast_to(tab[pl.ds(PHASES + phase[1, i], 1), :][:, : count * BLOCK], (8, count * BLOCK))
        base = jnp.broadcast_to(pltpu.roll(base, offset, 1)[:1], (BLOCK, count * BLOCK))
        col_op = pltpu.roll(base, 0, 1, stride=1, stride_axis=0).astype(BF16)
        window = jnp.dot(tall, col_op, preferred_element_type=F32).astype(BF16)
        for n in range(count):
            span = slice((block + n) * BLOCK, (block + n + 1) * BLOCK)
            part = window[:, n * BLOCK : (n + 1) * BLOCK]
            xbuf[:, span] = xbuf[:, span] + part if block + n in written else part
            written.add(block + n)

    def columns(p):
        for side in range(2):
            at = (2 * p + side) * BLOCK
            z = jnp.dot(xbuf[:, at : at + 2 * BLOCK], call[...], preferred_element_type=F32).astype(BF16)
            for k in range(NBASIS):
                zk = z[:, k * BLOCK : (k + 1) * BLOCK]
                for h in range(2):
                    at = DEPTH * h + NEED * k
                    zbuf[p % 2, at : at + NEED, side * BLOCK : (side + 1) * BLOCK] = zk[112 * h : 112 * h + NEED]

    def rows(p):
        got = [
            jnp.dot(
                rall[h, :, :DEPTH], zbuf[p % 2, DEPTH * h : DEPTH * (h + 1)], preferred_element_type=F32
            )
            for h in range(2)
        ]
        for strip in range(TILES):
            z, x = divmod(strip, 4)
            first = 64 * (z % 2) + 8 * x
            halves = [got[z // 2][first + 32 * c : first + 32 * c + 8] for c in range(2)]
            both = jnp.concatenate(halves, 0)
            if p == PAIRS - 1:
                row = lax.broadcasted_iota(jnp.int32, (STRIP, 2 * BLOCK), 0)
                lane = lax.broadcasted_iota(jnp.int32, (STRIP, 2 * BLOCK), 1)
                mark = jnp.zeros((STRIP, 2 * BLOCK), F32)
                for i in range(PIECES):
                    here = (row == i // 8) & (lane == META % (2 * BLOCK) + i % 8)
                    mark = jnp.where(here, dest[0, i].astype(F32), mark)
                both = jnp.where(lane >= META % (2 * BLOCK), mark, both)
            out[TILES - 1 - strip, :, 2 * p * BLOCK : 2 * (p + 1) * BLOCK] = both.astype(BF16)

    def rbuild():
        lane = lax.broadcasted_iota(jnp.int32, (BLOCK, H), 1)
        for h in range(2):
            for k in range(NBASIS):
                block, offset = divmod(NEED * k, BLOCK)
                base = jnp.broadcast_to(rowb[k : k + 1, :], (8, H))
                base = pltpu.roll(base, offset + STRIP * h, 1)
                band = pltpu.roll(jnp.broadcast_to(base[:1], (BLOCK, H)), 0, 1, stride=1, stride_axis=0)
                band = jnp.where((lane >= offset) & (lane < offset + NEED), band, 0.0).astype(BF16)
                for n in range(2):
                    span = slice((block + n) * BLOCK, (block + n + 1) * BLOCK)
                    part = band[:, n * BLOCK : (n + 1) * BLOCK]
                    rall[h, :, span] = rall[h, :, span] + part if n == 0 and offset else part

    def ready(p):
        while len(warped) < PIECES and STRIDE * len(warped) + HALF + 64 < (2 * p + 3) * BLOCK:
            warp(len(warped))
            warped.append(True)

    warped = []
    for i in range(AHEAD):
        lift(i)
    ready(0)
    for p in range(PAIRS + 1):
        if p < PAIRS:
            columns(p)
        if p == 0:
            rbuild()
        if p + 1 < PAIRS:
            ready(p + 1)
        if p > 0:
            rows(p - 1)


def place(goes, arr, out, main, left, right, words, dest, sem):
    upper = lax.rem(lax.axis_index("visit"), 2) == (0 if goes else 1)
    row = lax.broadcasted_iota(jnp.int32, (TILES, BLOCK), 0)
    lane = lax.broadcasted_iota(jnp.int32, (TILES, BLOCK), 1)
    low = high = jnp.zeros((TILES, BLOCK), F32)
    for s in range(TILES):
        tile = arr[s, :, COLS - BLOCK :].astype(F32)
        low = jnp.where(row == s, jnp.broadcast_to(tile[0:1], (TILES, BLOCK)), low)
        high = jnp.where(row == s, jnp.broadcast_to(tile[1:2], (TILES, BLOCK)), high)
    both = jnp.where(lane >= BLOCK - 8, low, pltpu.roll(high, BLOCK - 8, 1))
    words[...] = jnp.where(lane >= BLOCK - 16, both, 0.0).astype(jnp.int32)
    copy = pltpu.make_async_copy(words, dest, sem)
    copy.start()
    for buf in (main, left, right):
        buf[...] = jnp.zeros_like(buf)
    copy.wait()
    lane = lax.broadcasted_iota(jnp.int32, (8, BLOCK), 1)
    for s in range(TILES):
        z = s // 4
        for i in range(PIECES):
            q, o = divmod(STRIDE * i + REACH, BLOCK)

            def turned(b):
                block = arr[s, :, b * BLOCK : (b + 1) * BLOCK].astype(F32)
                return pltpu.roll(jnp.where(upper, block[8:], block[:8]), (BLOCK - o) % BLOCK, 1)

            first, second = turned(q), turned(q + 1)
            body = jnp.where(lane < BLOCK - o, first, second)
            low = first
            if o < REACH:
                low = jnp.where(lane < BLOCK - o, turned(q - 1), first)
            low = jnp.where(lane >= BLOCK - REACH, low, 0.0)
            high = second
            if o + REACH > BLOCK:
                high = jnp.where(lane < BLOCK - o, second, turned(q + 2))
            high = jnp.where(lane < REACH, high, 0.0)
            d = dest[s, BLOCK - 8 + i if i < 8 else BLOCK - 24 + i]
            for buf, at, part in ((main, d + 1, body), (left, d, low), (right, d + 2, high)):
                buf[at] = part if z == 0 else buf[at] + part

    def fill(j, carry):
        for u in range(4):
            pair = j * 4 + u
            sides = []
            for side in range(2):
                at = 2 * pair + side + 1
                sides.append(main[at] + left[at] + right[at])
            spot = TILES - 1 - j // 2 % 4 * 4 - j // 8
            out[8 * spot + j % 2 * 4 + u] = jnp.concatenate(sides, 0).astype(out.dtype)
        return carry

    lax.fori_loop(0, SKY // 8, fill, 0, unroll=2)


def gather(arr, out):
    for x in range(4):
        for u in range(8):
            terms = [arr[TILES - 1 - 4 * x - y, u].astype(F32) for y in range(4)]
            total = (terms[0] + terms[1]) + (terms[2] + terms[3])
            for side in range(2):
                at = (2 * u + side) * BLOCK
                out[8 * x : 8 * x + 8, at : at + BLOCK] = total[8 * side : 8 * side + 8]


def on_device(pixels, dest_block, phase_index, basis_row, basis_col, coefficients, visit_weight):
    vmem = pl.BlockSpec(memory_space=pltpu.VMEM)
    sent = pl.pallas_call(
        contribute,
        out_shape=jax.ShapeDtypeStruct((TILES, STRIP, COLS), BF16),
        in_specs=[pl.BlockSpec(memory_space=pltpu.HBM)] * 8,
        out_specs=vmem,
        scratch_shapes=[
            pltpu.SMEM((2, PIECES), jnp.int32),
            pltpu.SMEM((1, PIECES), jnp.int32),
            pltpu.SMEM((1, NBASIS), F32),
            pltpu.SMEM((8,), F32),
            pltpu.VMEM((2 * PHASES, 3 * BLOCK), F32),
            pltpu.VMEM((NBASIS, TAPS), BF16),
            pltpu.VMEM((NBASIS, TAPS), BF16),
            pltpu.VMEM((PIECES, H, BLOCK), BF16),
            pltpu.VMEM((H, NBASIS * BLOCK), BF16),
            pltpu.VMEM((2, BLOCK, 11 * BLOCK), BF16),
            pltpu.VMEM((H, COLS + BLOCK), BF16),
            pltpu.VMEM((2, 2 * DEPTH, 2 * BLOCK), BF16),
            pltpu.SemaphoreType.DMA((7,)),
            pltpu.SemaphoreType.DMA((PIECES // FETCH,)),
        ],
        compiler_params=pltpu.CompilerParams(vmem_limit_bytes=60 * 1024 * 1024),
    )(
        phase_index[0].T, dest_block, coefficients, visit_weight,
        jnp.asarray(bases()), basis_row, basis_col, pixels,
    )
    groups = [
        [(4 * y + x) * 8 + 2 * z + c for z in reversed(range(4)) for x in reversed(range(4))]
        for c in range(2) for y in range(4)
    ]
    arrived = lax.all_to_all(
        sent, ("tile", "visit"), split_axis=0, concat_axis=0, tiled=True, axis_index_groups=groups
    )

    def placed(goes):
        return pl.pallas_call(
            functools.partial(place, goes),
            out_shape=jax.ShapeDtypeStruct((SKY // 2, STRIP, BLOCK), BF16 if goes else F32),
            in_specs=[vmem],
            out_specs=vmem,
            scratch_shapes=[pltpu.VMEM((SKY + 2, 8, BLOCK), F32)] * 3
            + [
                pltpu.VMEM((TILES, BLOCK), jnp.int32),
                pltpu.SMEM((TILES, BLOCK), jnp.int32),
                pltpu.SemaphoreType.DMA,
            ],
            compiler_params=pltpu.CompilerParams(vmem_limit_bytes=40 * 1024 * 1024),
            cost_estimate=pl.CostEstimate(flops=10**7, bytes_accessed=4 * 10**6, transcendentals=0),
        )(arrived)

    sends, keeps = placed(True), placed(False)
    other = lax.ppermute(sends, "visit", [(i, i ^ 1) for i in range(8)])
    both = (keeps + other.astype(F32)).astype(BF16).reshape(TILES, 8, STRIP, BLOCK)
    backward = [
        [8 * (4 * y + x) + visit for x in reversed(range(4)) for y in reversed(range(4))]
        for visit in range(8)
    ]
    parts = lax.all_to_all(
        both, ("tile", "visit"), split_axis=0, concat_axis=0, tiled=True, axis_index_groups=backward
    )
    return pl.pallas_call(
        gather,
        out_shape=jax.ShapeDtypeStruct((32, 16 * BLOCK), F32),
        in_specs=[vmem],
        out_specs=vmem,
        compiler_params=pltpu.CompilerParams(vmem_limit_bytes=16 * 1024 * 1024),
    )(parts)


def solution(mesh):
    placed = (
        P("visit", "tile", None, None),
        P("visit", "tile"),
        P("visit", "tile", None),
        P(),
        P(),
        P("visit", None),
        P(),
    )
    return jax.shard_map(
        on_device, mesh=mesh, in_specs=placed, out_specs=P("visit", "tile"), check_vma=False
    )
```
